32 devices in a mesh: runs: 16 (over z, y, x), tm: 2 (over core).
Axes of the slice: x: 2, y: 2, z: 4, core: 2. Of those that a mesh axis runs over, the one named last changes fastest.
Arguments:
- tensor: bfloat16 [256, 32, 1024], P('runs', 'tm'), may hold values from 0 to 1
- run_counts: int32 [16], P('runs'), may hold values from 4 to 16, as said below
- run_init: float32 [256, 128], P('runs'), may hold values from 0.05 to 0.5
- bin_init: float32 [1024, 128], replicated, may hold values from 0.05 to 0.5
- time_init: float32 [32, 128], P('tm'), may hold values from 0.05 to 0.5
Outputs:
- run_factor: float32 [256, 128], P('runs')
- bin_factor: float32 [1024, 128], replicated
- time_factor: float32 [32, 128], P('tm')
The draws below stay inside these ranges and needn't reach their ends.
Inputs may be any that keep to these rules, and one draw needn't show every extreme that they name: `run_counts`: at most 16 live slots on an index of runs; some index has exactly 16.
All inputs are finite; a program needn't handle non-finite values.
Results may differ from the reference program's by a relative error of at most 0.0003.
Values sent between devices are 32-bit elements; how exact they have to be, the bound alone decides.
A program may use at most 64 MiB of HBM per device.

```python
import math
import jax
import jax.numpy as jnp
from jax import lax

ROWCAP = 16
J = 1024
R = 128
OUTER = 1
INNER = 1
RUNS_CAP = 256
TIMES = 32
N_RUNS = 16


def draw_run_counts(key, part):
    first = jax.random.fold_in(key, 11)
    second = jax.random.fold_in(key, 23)
    counts = jax.random.randint(first, (N_RUNS,), ROWCAP // 4, ROWCAP // 2 + 1)
    peak = jax.random.randint(second, (), 0, N_RUNS)
    position = jnp.arange(N_RUNS, dtype=jnp.int32)
    return jnp.where(position == peak, ROWCAP, counts).astype(jnp.int32)


def log_uniform(key, shape, lower, upper):
    exponent = jax.random.uniform(key, shape, jnp.float32, jnp.log(lower), jnp.log(upper))
    return jnp.exp(exponent)


def draw_tensor(key, part):
    components = 5 * R // 4
    run_key = jax.random.fold_in(key, 101)
    time_key = jax.random.fold_in(key, 103)
    centre_key = jax.random.fold_in(key, 104)
    breadth_key = jax.random.fold_in(key, 105)
    rough_key = jax.random.fold_in(key, 106)
    noise_key = jax.random.fold_in(key, 107)
    run_load = log_uniform(run_key, (RUNS_CAP, components), 0.02, 1.0)
    time_load = log_uniform(time_key, (TIMES, components), 0.02, 1.0)
    spread = 0.15
    divisor = 0.08 * components
    centre = jax.random.uniform(centre_key, (components,), jnp.float32, 0.0, 1.0)
    breadth = jax.random.uniform(breadth_key, (components,), jnp.float32, 0.05, 0.25)
    position = (jnp.arange(J, dtype=jnp.float32) + 0.5) / J
    profile = jnp.exp(-0.5 * ((position[:, None] - centre[None, :]) / breadth[None, :]) ** 2)
    roughness = jax.random.uniform(rough_key, (J, components), jnp.float32, 0.5, 1.5)
    spectra = (0.1 + profile) * roughness

    def single_run(index):
        loadings = time_load * run_load[index][None, :]
        signal = jnp.dot(loadings, spectra.T, precision=lax.Precision.HIGHEST)
        noise = jax.random.uniform(jax.random.fold_in(noise_key, index), (TIMES, J), jnp.float32, 1.0 - spread, 1.0 + spread)
        return jnp.clip(signal * noise / divisor, 0.0, 1.0)
    return lax.map(single_run, jnp.arange(RUNS_CAP, dtype=jnp.int32)).astype(jnp.bfloat16)


def level_of(stream_key, extent, shards, least, largest):
    gain = 1.0
    for dim, blocks in shards:
        heights = jax.random.uniform(jax.random.fold_in(jax.random.fold_in(stream_key, 6), dim), (blocks,), jnp.float32, least / len(shards), largest / len(shards))
        gain = gain * jnp.repeat(jnp.exp(heights), extent[dim] // blocks).reshape((-1,) + (1,) * (len(extent) - 1 - dim))
    return gain


def setup_inputs(seed: int = 0) -> dict:
    arg_keys = jax.random.split(jax.random.key(seed), 6)
    return {
        "tensor": draw_tensor(jax.random.fold_in(arg_keys[5], 71), 0),
        "run_counts": draw_run_counts(jax.random.fold_in(arg_keys[5], 71), 0),
        "run_init": jnp.clip(jnp.exp(math.log(0.5) - 2.3025851 * jax.random.uniform(arg_keys[2], (RUNS_CAP, R), jnp.float32) ** level_of(arg_keys[2], (RUNS_CAP, R), ((0, 16),), -0.2, 0.2)), 0.05, 0.5),
        "bin_init": jnp.clip(jnp.exp(jax.random.uniform(arg_keys[3], (J, R), jnp.float32, math.log(0.05), math.log(0.5))), 0.05, 0.5),
        "time_init": jnp.clip(jnp.exp(math.log(0.5) - 2.3025851 * jax.random.uniform(arg_keys[4], (TIMES, R), jnp.float32) ** level_of(arg_keys[4], (TIMES, R), ((0, 2),), -0.2, 0.2)), 0.05, 0.5),
    }


HIGH = lax.Precision.HIGHEST


def low(factor):
    return lax.optimization_barrier(factor.astype(jnp.bfloat16)).astype(jnp.float32)


def gram(factor):
    return jnp.dot(factor.T, factor, precision=HIGH)


def reference(tensor, run_counts, run_init, bin_init, time_init):
    slot = jnp.arange(RUNS_CAP, dtype=jnp.int32)
    owner = slot // ROWCAP
    live = ((slot % ROWCAP) < run_counts[owner]).astype(jnp.float32)[:, None]
    slabs = tensor.reshape(N_RUNS, ROWCAP, TIMES, J)
    runs = run_init * live
    bins = bin_init
    times = time_init
    run_gram = gram(runs)
    bin_gram = gram(bins)
    time_gram = gram(times)

    def bin_contract(bins_now):
        bins_low = low(bins_now)

        def one(slab):
            return jnp.einsum('ikj,jr->ikr', slab.astype(jnp.float32), bins_low, precision=HIGH)

        return lax.map(one, slabs).reshape(RUNS_CAP, TIMES, R)

    for outer in range(OUTER):
        for inner in range(INNER):
            inner_sum = bin_contract(bins)
            time_terms = jnp.einsum('ir,ikr->kr', runs, inner_sum, precision=HIGH)
            times = times * time_terms / jnp.dot(times, run_gram * bin_gram, precision=HIGH)
            time_gram = gram(times)
            times_low = low(times)
            run_slabs = runs.reshape(N_RUNS, ROWCAP, R)

            def bin_piece(pair):
                slab, rows = pair
                partial_value = jnp.einsum('ikj,kr->ijr', slab.astype(jnp.float32), times_low, precision=HIGH)
                return jnp.einsum('ir,ijr->jr', rows, partial_value, precision=HIGH)

            bin_terms = jnp.sum(lax.map(bin_piece, (slabs, run_slabs)), axis=0)
            bins = bins * bin_terms / jnp.dot(bins, run_gram * time_gram, precision=HIGH)
            bin_gram = gram(bins)
        inner_sum = bin_contract(bins)
        run_terms = jnp.einsum('kr,ikr->ir', times, inner_sum, precision=HIGH)
        runs = runs * run_terms / (jnp.dot(runs, bin_gram * time_gram, precision=HIGH) + 1.0 - live)
        run_gram = gram(runs)
    return runs, bins, times
```

```python
import functools

import jax
import jax.numpy as jnp
from jax import lax
from jax.experimental import pallas as pl
from jax.experimental.pallas import tpu as pltpu
from jax.sharding import PartitionSpec as P

HIGH = lax.Precision.HIGHEST
STEP_ROWS = 8
MESH = pl.DeviceIdType.MESH
F32 = jnp.float32
BF16 = jnp.bfloat16


def gram(factor):
    return jnp.dot(factor.T, factor, precision=HIGH)


def run_gram_sum(runs):
    return lax.psum(gram(runs), "runs")


def time_gram_sum(times):
    return lax.psum(gram(times), "tm")


def shards(tensor, run_counts, run_init, bin_init, time_init):
    rowcap = tensor.shape[0]
    count = run_counts[0]
    live = (jnp.arange(rowcap, dtype=jnp.int32) < count).astype(F32)[:, None]
    blocks = (count + STEP_ROWS - 1) // STEP_ROWS
    runs = run_init * live
    bins = bin_init
    times = time_init

    def sweep(step, init):
        return lax.fori_loop(0, blocks, lambda index, carry: step(index * STEP_ROWS, carry), init)

    run_gram = run_gram_sum(runs)
    bin_gram = gram(bins)
    bins_low = bins.astype(BF16)

    def step(start, total):
        block = lax.dynamic_slice_in_dim(tensor, start, STEP_ROWS, 0)
        rows = lax.dynamic_slice_in_dim(runs, start, STEP_ROWS, 0)
        inner_sum = jnp.einsum("ikj,jr->ikr", block, bins_low, preferred_element_type=F32)
        return total + jnp.einsum("ir,ikr->kr", rows, inner_sum, precision=HIGH)

    local = sweep(step, jnp.zeros((tensor.shape[1], bins.shape[1]), F32))
    time_terms = lax.psum(local, "runs")
    times = times * time_terms / jnp.dot(times, run_gram * bin_gram, precision=HIGH)
    time_gram = time_gram_sum(times)
    times_low = times.astype(BF16)

    def step(start, total):
        block = lax.dynamic_slice_in_dim(tensor, start, STEP_ROWS, 0)
        rows = lax.dynamic_slice_in_dim(runs, start, STEP_ROWS, 0)
        partial_value = jnp.einsum("ikj,kr->ijr", block, times_low, preferred_element_type=F32)
        return total + jnp.einsum("ir,ijr->jr", rows, partial_value, precision=HIGH)

    local_terms = sweep(step, jnp.zeros((tensor.shape[2], times.shape[1]), F32))
    mixing = run_gram * time_gram
    bin_terms = lax.psum(local_terms, ("runs", "tm"))
    bins = bins * bin_terms / jnp.dot(bins, mixing, precision=HIGH)
    bin_gram = gram(bins)
    run_bins_low = bins.astype(BF16)

    def step(start, total):
        block = lax.dynamic_slice_in_dim(tensor, start, STEP_ROWS, 0)
        inner_sum = jnp.einsum("ikj,jr->ikr", block, run_bins_low, preferred_element_type=F32)
        row_terms = jnp.einsum("kr,ikr->ir", times, inner_sum, precision=HIGH)
        return lax.dynamic_update_slice_in_dim(total, row_terms, start, 0)

    local = sweep(step, jnp.zeros((rowcap, bins.shape[1]), F32))
    run_terms = lax.psum(local, "tm")
    runs = runs * run_terms / (jnp.dot(runs, bin_gram * time_gram, precision=HIGH) + 1.0 - live)
    return (runs, bins, times)


def dot_t(a, b):
    return lax.dot_general(
        a, b, (((0,), (0,)), ((), ())), precision=HIGH, preferred_element_type=F32
    )


def dot_f32(a, b):
    return lax.dot_general(
        a, b, (((1,), (0,)), ((), ())), precision=HIGH, preferred_element_type=F32
    )


def dot_low(a, b):
    return lax.dot_general(a, b, (((1,), (0,)), ((), ())), preferred_element_type=F32)


def split(x):
    hi = x.astype(BF16)
    return hi, (x - hi.astype(F32)).astype(BF16)


def kernel(
    n, m, count_ref, tensor_ref, run_ref, bin_ref, time_ref,
    run_out, bin_out, time_out,
    wide, wide_in, flipped, terms, terms_in, bins_all, halves, parts, parts_in,
    times_all, times_flat,
    wide_s, wide_r, half_s, half_r, fwd_s, fwd_r, part_s, part_r, row_s, row_r,
    term_s, term_r, bin_s, bin_r, pass_s, pass_r, out_sem,
):
    me = lax.axis_index("runs")
    tm = lax.axis_index("tm")
    rows = run_ref.shape[0]
    kk = time_ref.shape[0]
    jj, rank = bin_ref.shape
    block = jj // (n * m)
    half = rows // m
    span = jj // m
    flat = tm * n + me

    def copy(src, dst, send, recv, run_index, tm_index):
        made = pltpu.make_async_remote_copy(
            src_ref=src, dst_ref=dst, send_sem=send, recv_sem=recv,
            device_id=(run_index, tm_index), device_id_type=MESH,
        )
        made.start()
        return made

    barrier = pltpu.get_barrier_semaphore()
    for off in range(1, n * m):
        peer = lax.rem(flat + off, n * m)
        pl.semaphore_signal(
            barrier, inc=1, device_id=(lax.rem(peer, n), peer // n), device_id_type=MESH
        )

    live = (lax.broadcasted_iota(jnp.int32, (rows, rank), 0) < count_ref[0]).astype(F32)
    runs = run_ref[...] * live
    halves[flat] = jnp.where(tm == 0, runs[:half], runs[rows - half:]) if m == 2 else runs
    tensor = tensor_ref[...]
    wide[...] = tensor.astype(F32)
    times = time_ref[...]
    inner = dot_low(tensor, bin_ref[...].astype(BF16)).reshape(rows, kk, rank)
    upper = inner[0] * runs[0:1]
    for i in range(1, rows):
        upper = upper + inner[i] * runs[i:i + 1]
    lower = dot_f32(times, dot_t(runs, runs) * dot_t(bin_ref[...], bin_ref[...]))
    both = jnp.concatenate([upper, lower], axis=1)
    for k in range(kk):
        parts[k] = both[k:k + 1]

    pl.semaphore_wait(barrier, n * m - 1)

    part_copies = []
    for off in range(1, n):
        peer = lax.rem(me + off, n)
        part_copies.append(
            copy(parts.at[peer], parts_in.at[off], part_s.at[off], part_r.at[off], peer, tm)
        )
    wide_copies = []
    for off in range(1, m):
        peer = lax.rem(tm + off, m)
        wide_copies.append(
            copy(wide, wide_in.at[off], wide_s.at[off], wide_r.at[off], me, peer)
        )
    half_copies = []
    for off in range(1, n):
        peer = lax.rem(me + off, n)
        half_copies.append(
            copy(halves.at[flat], halves.at[flat], half_s.at[off], half_r.at[off], peer, tm)
        )

    start = pl.multiple_of(tm * span, span)
    flipped[:, : rows * kk] = wide[:, pl.ds(start, span)].T.astype(BF16)

    total = parts[me]
    for made, off in zip(part_copies, range(1, n)):
        made.wait_recv()
        total = total + parts_in[off]
    times_all[flat] = time_ref[pl.ds(me, 1), :] * total[:, :rank] / total[:, rank:]
    row_copies = []
    for off in range(1, n * m):
        peer = lax.rem(flat + off, n * m)
        row_copies.append(
            copy(
                times_all.at[flat], times_all.at[flat], row_s.at[off], row_r.at[off],
                lax.rem(peer, n), peer // n,
            )
        )
    for made in half_copies:
        made.wait_recv()
    fwd_copies = []
    mine = pl.ds(tm * n, n)
    for off in range(1, m):
        peer = lax.rem(tm + off, m)
        fwd_copies.append(
            copy(halves.at[mine], halves.at[mine], fwd_s.at[off], fwd_r.at[off], me, peer)
        )
    for off in range(1, m):
        wide_copies[off - 1].wait_recv()
        flipped[:, off * rows * kk:(off + 1) * rows * kk] = (
            wide_in[off, :, pl.ds(start, span)].T.astype(BF16)
        )
    for made in fwd_copies:
        made.wait_recv()
    every = halves[...].reshape(n * m * half, rank)
    run_gram = dot_t(every, every)
    for made in row_copies:
        made.wait_recv()
    for k in range(n * m):
        times_flat[k:k + 1, :] = times_all[k]

    weights = []
    for off in range(m):
        index = lax.rem(tm + off, m)
        low = times_flat[pl.ds(pl.multiple_of(index * kk, kk), kk), :].astype(BF16).astype(F32)
        weights.extend(low * runs[i:i + 1] for i in range(rows))
    hi, lo = split(jnp.concatenate(weights, axis=0))
    product = dot_low(flipped[...], jnp.concatenate([hi, lo], axis=1))
    terms[...] = (product[:, :rank] + product[:, rank:]).reshape(n, block, rank)
    term_copies = []
    for off in range(1, n):
        peer = lax.rem(me + off, n)
        term_copies.append(
            copy(terms.at[peer], terms_in.at[off], term_s.at[off], term_r.at[off], peer, tm)
        )
    every_time = times_flat[...]
    time_gram = dot_t(every_time, every_time)
    own = bin_ref[pl.ds(pl.multiple_of(flat * block, block), block), :]
    scale = own / dot_f32(own, run_gram * time_gram)
    total = terms[me]
    for made, off in zip(term_copies, range(1, n)):
        made.wait_recv()
        total = total + terms_in[off]
    bins_all[flat] = scale * total

    bin_copies = []
    for off in range(1, n):
        peer = lax.rem(me + off, n)
        bin_copies.append(
            copy(bins_all.at[flat], bins_all.at[flat], bin_s.at[off], bin_r.at[off], peer, tm)
        )
    pass_copies = []
    for step in range(n):
        if step > 0:
            bin_copies[step - 1].wait_recv()
        source = tm * n + lax.rem(me - step + n, n)
        for off in range(1, m):
            peer = lax.rem(tm + off, m)
            pass_copies.append(
                copy(
                    bins_all.at[source], bins_all.at[source],
                    pass_s.at[step, off], pass_r.at[step, off], me, peer,
                )
            )
    for made in pass_copies:
        made.wait_recv()
    write = pltpu.make_async_copy(bins_all, bin_out, out_sem)
    write.start()
    bins = bins_all[...].reshape(jj, rank)
    bins_low = bins.astype(BF16)
    run_terms = None
    for off in range(m):
        index = lax.rem(tm + off, m)
        slab = tensor_ref[...] if off == 0 else wide_in[off].astype(BF16)
        inner = dot_low(slab, bins_low).reshape(rows, kk, rank)
        weight = times_flat[pl.ds(pl.multiple_of(index * kk, kk), kk), :]
        some = jnp.sum(inner * weight[None], axis=1)
        run_terms = some if run_terms is None else run_terms + some
    mixing = dot_t(bins, bins) * time_gram
    run_out[...] = runs * run_terms / (dot_f32(runs, mixing) + 1.0 - live)
    time_out[...] = times_flat[pl.ds(pl.multiple_of(tm * kk, kk), kk), :]

    for made in (
        part_copies + wide_copies + half_copies + row_copies + fwd_copies
        + term_copies + bin_copies + pass_copies
    ):
        made.wait_send()
    write.wait()


def fused(n, m, tensor, run_counts, run_init, bin_init, time_init):
    rows, kk, jj = tensor.shape
    rank = bin_init.shape[1]
    block = jj // (n * m)
    half = rows // m
    dma = pltpu.SemaphoreType.DMA
    vmem = pl.BlockSpec(memory_space=pltpu.VMEM)
    runs, bins, times = pl.pallas_call(
        functools.partial(kernel, n, m),
        out_shape=(
            jax.ShapeDtypeStruct((rows, rank), F32),
            jax.ShapeDtypeStruct((n * m, block, rank), F32),
            jax.ShapeDtypeStruct((kk, rank), F32),
        ),
        in_specs=[pl.BlockSpec(memory_space=pltpu.SMEM)] + [vmem] * 4,
        out_specs=(vmem, pl.BlockSpec(memory_space=pl.ANY), vmem),
        scratch_shapes=[
            pltpu.VMEM((rows * kk, jj), F32),
            pltpu.VMEM((m, rows * kk, jj), F32),
            pltpu.VMEM((jj // m, m * rows * kk), BF16),
            pltpu.VMEM((n, block, rank), F32),
            pltpu.VMEM((n, block, rank), F32),
            pltpu.VMEM((n * m, block, rank), F32),
            pltpu.VMEM((n * m, half, rank), F32),
            pltpu.VMEM((n, 1, 2 * rank), F32),
            pltpu.VMEM((n, 1, 2 * rank), F32),
            pltpu.VMEM((n * m, 1, rank), F32),
            pltpu.VMEM((n * m, rank), F32),
            dma((m,)), dma((m,)), dma((n,)), dma((n,)), dma((m,)), dma((m,)),
            dma((n,)), dma((n,)), dma((n * m,)), dma((n * m,)),
            dma((n,)), dma((n,)), dma((n,)), dma((n,)), dma((n, m)), dma((n, m)), dma,
        ],
        compiler_params=pltpu.CompilerParams(
            collective_id=0, has_side_effects=True, vmem_limit_bytes=40 * 2**20
        ),
    )(run_counts, tensor.reshape(rows * kk, jj), run_init, bin_init, time_init)
    return runs, bins.reshape(jj, rank), times


def update(n, m, *args):
    rows, kk, jj = args[0].shape
    fits = m == 2 and kk == n and kk % 16 == 0 and rows % (8 * m) == 0 and jj % (8 * n * m) == 0
    return fused(n, m, *args) if fits else shards(*args)


def solution(mesh):
    return jax.shard_map(
        functools.partial(update, mesh.shape["runs"], mesh.shape["tm"]),
        mesh=mesh,
        in_specs=(P("runs", "tm", None), P("runs"), P("runs", None), P(), P("tm", None)),
        out_specs=(P("runs", None), P(), P("tm", None)),
        check_vma=False,
    )
```

```python
import functools

import jax
import jax.numpy as jnp
from jax import lax
from jax.experimental import pallas as pl
from jax.experimental.pallas import tpu as pltpu
from jax.sharding import PartitionSpec as P

HIGH = lax.Precision.HIGHEST
STEP_ROWS = 8
MESH = pl.DeviceIdType.MESH
F32 = jnp.float32
BF16 = jnp.bfloat16


def gram(factor):
    return jnp.dot(factor.T, factor, precision=HIGH)


def run_gram_sum(runs):
    return lax.psum(gram(runs), "runs")


def time_gram_sum(times):
    return lax.psum(gram(times), "tm")


def shards(tensor, run_counts, run_init, bin_init, time_init):
    rowcap = tensor.shape[0]
    count = run_counts[0]
    live = (jnp.arange(rowcap, dtype=jnp.int32) < count).astype(F32)[:, None]
    blocks = (count + STEP_ROWS - 1) // STEP_ROWS
    runs = run_init * live
    bins = bin_init
    times = time_init

    def sweep(step, init):
        return lax.fori_loop(0, blocks, lambda index, carry: step(index * STEP_ROWS, carry), init)

    run_gram = run_gram_sum(runs)
    bin_gram = gram(bins)
    bins_low = bins.astype(BF16)

    def step(start, total):
        block = lax.dynamic_slice_in_dim(tensor, start, STEP_ROWS, 0)
        rows = lax.dynamic_slice_in_dim(runs, start, STEP_ROWS, 0)
        inner_sum = jnp.einsum("ikj,jr->ikr", block, bins_low, preferred_element_type=F32)
        return total + jnp.einsum("ir,ikr->kr", rows, inner_sum, precision=HIGH)

    local = sweep(step, jnp.zeros((tensor.shape[1], bins.shape[1]), F32))
    time_terms = lax.psum(local, "runs")
    times = times * time_terms / jnp.dot(times, run_gram * bin_gram, precision=HIGH)
    time_gram = time_gram_sum(times)
    times_low = times.astype(BF16)

    def step(start, total):
        block = lax.dynamic_slice_in_dim(tensor, start, STEP_ROWS, 0)
        rows = lax.dynamic_slice_in_dim(runs, start, STEP_ROWS, 0)
        partial_value = jnp.einsum("ikj,kr->ijr", block, times_low, preferred_element_type=F32)
        return total + jnp.einsum("ir,ijr->jr", rows, partial_value, precision=HIGH)

    local_terms = sweep(step, jnp.zeros((tensor.shape[2], times.shape[1]), F32))
    mixing = run_gram * time_gram
    bin_terms = lax.psum(local_terms, ("runs", "tm"))
    bins = bins * bin_terms / jnp.dot(bins, mixing, precision=HIGH)
    bin_gram = gram(bins)
    run_bins_low = bins.astype(BF16)

    def step(start, total):
        block = lax.dynamic_slice_in_dim(tensor, start, STEP_ROWS, 0)
        inner_sum = jnp.einsum("ikj,jr->ikr", block, run_bins_low, preferred_element_type=F32)
        row_terms = jnp.einsum("kr,ikr->ir", times, inner_sum, precision=HIGH)
        return lax.dynamic_update_slice_in_dim(total, row_terms, start, 0)

    local = sweep(step, jnp.zeros((rowcap, bins.shape[1]), F32))
    run_terms = lax.psum(local, "tm")
    runs = runs * run_terms / (jnp.dot(runs, bin_gram * time_gram, precision=HIGH) + 1.0 - live)
    return (runs, bins, times)


def split(x):
    hi = x.astype(BF16)
    return hi, (x - hi.astype(F32)).astype(BF16)


def dot_low(a, b):
    return lax.dot_general(a, b, (((1,), (0,)), ((), ())), preferred_element_type=F32)


def fold(x):
    half = x.shape[1] // 2
    return x[:, :half] + x[:, half:]


def self_gram(x):
    both = jnp.concatenate(split(x), axis=1)
    product = fold(
        lax.dot_general(both, both, (((0,), (0,)), ((), ())), preferred_element_type=F32)
    )
    half = product.shape[0] // 2
    return product[:half] + product[half:]


def dot_f32(a, b):
    right = jnp.concatenate(split(b), axis=1)
    return fold(
        dot_low(jnp.concatenate(split(a), axis=1), jnp.concatenate([right, right], axis=0))
    )


QUAD = 4
VMEM_LIMIT = 64 * 2**20 - 2**16


def kernel(
    n, m, count_in, tensor_in, run_in, bin_in, time_in,
    run_out, bin_out, time_out,
    count_ref, slabs, run_ref, bin_ref, time_ref,
    wide, wide_in, flipped, terms, terms_one, terms_mid, terms_two, terms_last, terms_three,
    bins_all, inner_sum, halves, parts, parts_in, times_all, times_flat,
    load_sem, wide_s, wide_r, half_s, half_r, fwd_s, fwd_r, part_s, part_r, row_s, row_r,
    one_s, one_r, two_s, two_r, three_s, three_r,
    z_s, z_r, near_s, near_r, far_s, far_r, pass_s, pass_r, out_sem,
):
    me = lax.axis_index("runs")
    tm = lax.axis_index("tm")
    rows = run_ref.shape[0]
    kk = time_ref.shape[0]
    jj, rank = bin_ref.shape
    block = jj // (n * m)
    half = rows // m
    span = jj // m
    flat = tm * n + me
    zs = n // QUAD
    strip = QUAD * block

    z = me // QUAD
    first = 2 - tm
    second = 1 + tm
    bit_one = lax.rem(me // first, 2)
    bit_two = lax.rem(me // second, 2)
    partner_one = me + first * (1 - 2 * bit_one)
    partner_two = me + second * (1 - 2 * bit_two)

    def place(z_index, flip_one, flip_two):
        one = 1 - bit_one if flip_one else bit_one
        two = 1 - bit_two if flip_two else bit_two
        return z_index * QUAD + one * first + two * second

    def copy(src, dst, send, recv, run_index, tm_index):
        made = pltpu.make_async_remote_copy(
            src_ref=src, dst_ref=dst, send_sem=send, recv_sem=recv,
            device_id=(run_index, tm_index), device_id_type=MESH,
        )
        made.start()
        return made

    loads = [
        pltpu.make_async_copy(src, dst, load_sem.at[index])
        for index, (src, dst) in enumerate((
            (tensor_in, slabs.at[0]), (bin_in, bin_ref), (count_in, count_ref),
            (run_in, run_ref), (time_in, time_ref),
        ))
    ]
    for made in loads:
        made.start()

    barrier = pltpu.get_barrier_semaphore()
    for off in range(1, n * m):
        peer = lax.rem(flat + off, n * m)
        pl.semaphore_signal(
            barrier, inc=1, device_id=(lax.rem(peer, n), peer // n), device_id_type=MESH
        )
    for made in loads:
        made.wait()

    live = (lax.broadcasted_iota(jnp.int32, (rows, rank), 0) < count_ref[0]).astype(F32)
    runs = run_ref[...] * live
    halves[flat] = jnp.where(tm == 0, runs[:half], runs[rows - half:])
    tensor = slabs[0]
    times = time_ref[...]
    inner = dot_low(tensor, bin_ref[...].astype(BF16)).reshape(rows, kk, rank)
    upper = inner[0] * runs[0:1]
    for i in range(1, rows):
        upper = upper + inner[i] * runs[i:i + 1]
    lower = dot_f32(times, self_gram(runs) * self_gram(bin_ref[...]))
    both = jnp.concatenate([upper, lower], axis=1)
    for k in range(kk):
        parts[k] = both[k:k + 1]

    pl.semaphore_wait(barrier, n * m - 1)

    part_copies = []
    for off in range(1, n):
        peer = lax.rem(me + off, n)
        part_copies.append(
            copy(parts.at[peer], parts_in.at[off], part_s.at[off], part_r.at[off], peer, tm)
        )
    wide[...] = tensor.astype(F32)
    wide_copies = []
    for off in range(1, m):
        peer = lax.rem(tm + off, m)
        wide_copies.append(
            copy(wide, wide_in.at[off], wide_s.at[off], wide_r.at[off], me, peer)
        )
    half_copies = []
    for off in range(1, n):
        peer = lax.rem(me + off, n)
        half_copies.append(
            copy(halves.at[flat], halves.at[flat], half_s.at[off], half_r.at[off], peer, tm)
        )

    start = pl.multiple_of(tm * span, span)
    flipped[:, : rows * kk] = wide[:, pl.ds(start, span)].T.astype(BF16)

    total = parts[me]
    for made, off in zip(part_copies, range(1, n)):
        made.wait_recv()
        total = total + parts_in[off]
    times_all[flat] = time_ref[pl.ds(me, 1), :] * total[:, :rank] / total[:, rank:]
    row_copies = []
    for off in range(1, n * m):
        peer = lax.rem(flat + off, n * m)
        row_copies.append(
            copy(
                times_all.at[flat], times_all.at[flat], row_s.at[off], row_r.at[off],
                lax.rem(peer, n), peer // n,
            )
        )
    for made in half_copies:
        made.wait_recv()
    fwd_copies = []
    mine = pl.ds(tm * n, n)
    for off in range(1, m):
        peer = lax.rem(tm + off, m)
        fwd_copies.append(
            copy(halves.at[mine], halves.at[mine], fwd_s.at[off], fwd_r.at[off], me, peer)
        )
    for off in range(1, m):
        wide_copies[off - 1].wait_recv()
        slabs[off] = wide_in[off].astype(BF16)
        flipped[:, off * rows * kk:(off + 1) * rows * kk] = (
            wide_in[off, :, pl.ds(start, span)].T.astype(BF16)
        )
    for made in row_copies:
        made.wait_recv()
    for k in range(n * m):
        times_flat[k:k + 1, :] = times_all[k]

    weights = []
    for off in range(m):
        index = lax.rem(tm + off, m)
        low = times_flat[pl.ds(pl.multiple_of(index * kk, kk), kk), :].astype(BF16).astype(F32)
        weights.extend(low * runs[i:i + 1] for i in range(rows))
    weight = jnp.concatenate(split(jnp.concatenate(weights, axis=0)), axis=1)
    order = list(range(1, zs)) + [0]
    z_of = [lax.rem(z + k, zs) for k in range(zs)]
    one_copies = {}
    for k in order:
        piece = flipped[pl.ds(pl.multiple_of(z_of[k] * strip, strip), strip), :]
        terms[pl.ds(z_of[k] * QUAD, QUAD)] = fold(dot_low(piece, weight)).reshape(
            QUAD, block, rank
        )
        for flip in (1, 0):
            one_copies[k, flip] = copy(
                terms.at[place(z_of[k], 1, flip)], terms_one.at[k, flip],
                one_s.at[k, flip], one_r.at[k, flip], partner_one, tm,
            )
    two_copies = {}
    for k in order:
        one_copies[k, 1].wait_recv()
        terms_mid[k] = terms[place(z_of[k], 0, 1)] + terms_one[k, 1]
        two_copies[k] = copy(
            terms_mid.at[k], terms_two.at[k], two_s.at[k], two_r.at[k], partner_two, tm
        )
    for made in fwd_copies:
        made.wait_recv()
    run_gram = self_gram(halves[...].reshape(n * m * half, rank))
    time_gram = self_gram(times_flat[...])
    own = bin_ref[pl.ds(pl.multiple_of(flat * block, block), block), :]
    scale = own / dot_f32(own, run_gram * time_gram)
    three_copies = {}
    for k in order:
        one_copies[k, 0].wait_recv()
        two_copies[k].wait_recv()
        terms_last[k] = terms[place(z_of[k], 0, 0)] + terms_one[k, 0] + terms_two[k]
        if k > 0:
            three_copies[k] = copy(
                terms_last.at[k], terms_three.at[k], three_s.at[k], three_r.at[k],
                place(z_of[k], 0, 0), tm,
            )
    total = terms_last[0]
    for k in range(1, zs):
        three_copies[k].wait_recv()
        total = total + terms_three[k]
    bins_all[flat] = scale * total

    z_copies = {}
    for k in range(1, zs):
        z_copies[k] = copy(
            bins_all.at[flat], bins_all.at[flat], z_s.at[k], z_r.at[k],
            place(z_of[k], 0, 0), tm,
        )
    from_z = [lax.rem(z - k + zs, zs) for k in range(zs)]
    near_copies, far_copies, pass_copies = {}, {}, {}

    def send_on(store, key, slot, sends, recvs, run_index, tm_index):
        store[key] = copy(
            bins_all.at[slot], bins_all.at[slot], sends.at[key], recvs.at[key],
            run_index, tm_index,
        )

    other = lax.rem(tm + 1, m)
    for k in range(zs):
        if k > 0:
            z_copies[k].wait_recv()
        slot = tm * n + place(from_z[k], 0, 0)
        send_on(near_copies, k, slot, near_s, near_r, partner_two, tm)
        send_on(far_copies, (k, 0), slot, far_s, far_r, partner_one, tm)
        send_on(pass_copies, (k, 0), slot, pass_s, pass_r, me, other)
    for k in range(zs):
        near_copies[k].wait_recv()
        slot = tm * n + place(from_z[k], 0, 1)
        send_on(far_copies, (k, 1), slot, far_s, far_r, partner_one, tm)
        send_on(pass_copies, (k, 1), slot, pass_s, pass_r, me, other)
    for k in range(zs):
        for flip in (0, 1):
            far_copies[k, flip].wait_recv()
            slot = tm * n + place(from_z[k], 1, flip)
            send_on(pass_copies, (k, 2 + flip), slot, pass_s, pass_r, me, other)
    bin_gram = None
    writes = []
    for k in range(zs):
        for index in range(QUAD):
            pass_copies[k, index].wait_recv()
        pieces = []
        for core in range(m):
            mine = pl.ds(core * n + from_z[k] * QUAD, QUAD)
            pieces.append(bins_all[mine].reshape(strip, rank))
            made = pltpu.make_async_copy(
                bins_all.at[mine], bin_out.at[mine], out_sem.at[k, core]
            )
            made.start()
            writes.append(made)
        bins = jnp.concatenate(pieces, axis=0)
        bins_low = bins.astype(BF16)
        some = self_gram(bins)
        bin_gram = some if k == 0 else bin_gram + some
        for off in range(m):
            slab = jnp.concatenate(
                [
                    slabs[off, :, pl.ds(pl.multiple_of(core * span + from_z[k] * strip, strip), strip)]
                    for core in range(m)
                ],
                axis=1,
            )
            product = dot_low(slab, bins_low)
            inner_sum[off] = product if k == 0 else inner_sum[off] + product
    run_terms = None
    for off in range(m):
        index = lax.rem(tm + off, m)
        weight = times_flat[pl.ds(pl.multiple_of(index * kk, kk), kk), :]
        some = jnp.sum(inner_sum[off].reshape(rows, kk, rank) * weight[None], axis=1)
        run_terms = some if run_terms is None else run_terms + some
    run_out[...] = runs * run_terms / (dot_f32(runs, bin_gram * time_gram) + 1.0 - live)
    time_out[...] = times_flat[pl.ds(pl.multiple_of(tm * kk, kk), kk), :]

    for made in part_copies + wide_copies + half_copies + row_copies + fwd_copies:
        made.wait_send()
    for store in (
        one_copies, two_copies, three_copies, z_copies, near_copies, far_copies, pass_copies
    ):
        for made in store.values():
            made.wait_send()
    for made in writes:
        made.wait()


def hand_out(*refs):
    count = (len(refs) - 1) // 2
    sems = refs[-1]
    copies = [
        pltpu.make_async_copy(refs[i], refs[count + i], sems.at[i]) for i in range(count)
    ]
    for made in copies:
        made.start()
    for made in copies:
        made.wait()


def fused(n, m, tensor, run_counts, run_init, bin_init, time_init):
    rows, kk, jj = tensor.shape
    rank = bin_init.shape[1]
    block = jj // (n * m)
    half = rows // m
    zs = n // QUAD
    dma = pltpu.SemaphoreType.DMA
    vmem = pl.BlockSpec(memory_space=pltpu.VMEM)
    anywhere = pl.BlockSpec(memory_space=pl.ANY)
    shapes = (
        jax.ShapeDtypeStruct((rows, rank), F32),
        jax.ShapeDtypeStruct((n * m, block, rank), F32),
        jax.ShapeDtypeStruct((kk, rank), F32),
    )
    results = pl.pallas_call(
        functools.partial(kernel, n, m),
        out_shape=shapes,
        in_specs=[anywhere] * 5,
        out_specs=(vmem, anywhere, vmem),
        scratch_shapes=[
            pltpu.SMEM((1,), jnp.int32),
            pltpu.VMEM((m, rows * kk, jj), BF16),
            pltpu.VMEM((rows, rank), F32),
            pltpu.VMEM((jj, rank), F32),
            pltpu.VMEM((kk, rank), F32),
            pltpu.VMEM((rows * kk, jj), F32),
            pltpu.VMEM((m, rows * kk, jj), F32),
            pltpu.VMEM((jj // m, m * rows * kk), BF16),
            pltpu.VMEM((n, block, rank), F32),
            pltpu.VMEM((zs, 2, block, rank), F32),
            pltpu.VMEM((zs, block, rank), F32),
            pltpu.VMEM((zs, block, rank), F32),
            pltpu.VMEM((zs, block, rank), F32),
            pltpu.VMEM((zs, block, rank), F32),
            pltpu.VMEM((n * m, block, rank), F32),
            pltpu.VMEM((m, rows * kk, rank), F32),
            pltpu.VMEM((n * m, half, rank), F32),
            pltpu.VMEM((n, 1, 2 * rank), F32),
            pltpu.VMEM((n, 1, 2 * rank), F32),
            pltpu.VMEM((n * m, 1, rank), F32),
            pltpu.VMEM((n * m, rank), F32),
            dma((5,)), dma((m,)), dma((m,)), dma((n,)), dma((n,)), dma((m,)), dma((m,)),
            dma((n,)), dma((n,)), dma((n * m,)), dma((n * m,)),
            dma((zs, 2)), dma((zs, 2)), dma((zs,)), dma((zs,)), dma((zs,)), dma((zs,)),
            dma((zs,)), dma((zs,)), dma((zs,)), dma((zs,)), dma((zs, 2)), dma((zs, 2)),
            dma((zs, QUAD)), dma((zs, QUAD)), dma((zs, m)),
        ],
        compiler_params=pltpu.CompilerParams(
            collective_id=0, has_side_effects=True, vmem_limit_bytes=VMEM_LIMIT
        ),
    )(run_counts, tensor.reshape(rows * kk, jj), run_init, bin_init, time_init)
    runs, bins, times = pl.pallas_call(
        hand_out,
        out_shape=shapes,
        in_specs=[anywhere] * 3,
        out_specs=[anywhere] * 3,
        scratch_shapes=[dma((3,))],
        compiler_params=pltpu.CompilerParams(vmem_limit_bytes=VMEM_LIMIT),
    )(*results)
    return runs, bins.reshape(jj, rank), times


def update(n, m, *args):
    rows, kk, jj = args[0].shape
    fits = m == 2 and kk == n and n % QUAD == 0 and kk % 16 == 0 and rows % (8 * m) == 0
    fits = fits and jj % (8 * n * m) == 0 and (QUAD * jj // (n * m)) % 128 == 0
    return fused(n, m, *args) if fits else shards(*args)


def solution(mesh):
    return jax.shard_map(
        functools.partial(update, mesh.shape["runs"], mesh.shape["tm"]),
        mesh=mesh,
        in_specs=(P("runs", "tm", None), P("runs"), P("runs", None), P(), P("tm", None)),
        out_specs=(P("runs", None), P(), P("tm", None)),
        check_vma=False,
    )
```

```python
import functools

import jax
import jax.numpy as jnp
from jax import lax
from jax.experimental import pallas as pl
from jax.experimental.pallas import tpu as pltpu
from jax.sharding import PartitionSpec as P

HIGH = lax.Precision.HIGHEST
STEP_ROWS = 8
MESH = pl.DeviceIdType.MESH
F32 = jnp.float32
BF16 = jnp.bfloat16


def gram(factor):
    return jnp.dot(factor.T, factor, precision=HIGH)


def run_gram_sum(runs):
    return lax.psum(gram(runs), "runs")


def time_gram_sum(times):
    return lax.psum(gram(times), "tm")


def shards(tensor, run_counts, run_init, bin_init, time_init):
    rowcap = tensor.shape[0]
    count = run_counts[0]
    live = (jnp.arange(rowcap, dtype=jnp.int32) < count).astype(F32)[:, None]
    blocks = (count + STEP_ROWS - 1) // STEP_ROWS
    runs = run_init * live
    bins = bin_init
    times = time_init

    def sweep(step, init):
        return lax.fori_loop(0, blocks, lambda index, carry: step(index * STEP_ROWS, carry), init)

    run_gram = run_gram_sum(runs)
    bin_gram = gram(bins)
    bins_low = bins.astype(BF16)

    def step(start, total):
        block = lax.dynamic_slice_in_dim(tensor, start, STEP_ROWS, 0)
        rows = lax.dynamic_slice_in_dim(runs, start, STEP_ROWS, 0)
        inner_sum = jnp.einsum("ikj,jr->ikr", block, bins_low, preferred_element_type=F32)
        return total + jnp.einsum("ir,ikr->kr", rows, inner_sum, precision=HIGH)

    local = sweep(step, jnp.zeros((tensor.shape[1], bins.shape[1]), F32))
    time_terms = lax.psum(local, "runs")
    times = times * time_terms / jnp.dot(times, run_gram * bin_gram, precision=HIGH)
    time_gram = time_gram_sum(times)
    times_low = times.astype(BF16)

    def step(start, total):
        block = lax.dynamic_slice_in_dim(tensor, start, STEP_ROWS, 0)
        rows = lax.dynamic_slice_in_dim(runs, start, STEP_ROWS, 0)
        partial_value = jnp.einsum("ikj,kr->ijr", block, times_low, preferred_element_type=F32)
        return total + jnp.einsum("ir,ijr->jr", rows, partial_value, precision=HIGH)

    local_terms = sweep(step, jnp.zeros((tensor.shape[2], times.shape[1]), F32))
    mixing = run_gram * time_gram
    bin_terms = lax.psum(local_terms, ("runs", "tm"))
    bins = bins * bin_terms / jnp.dot(bins, mixing, precision=HIGH)
    bin_gram = gram(bins)
    run_bins_low = bins.astype(BF16)

    def step(start, total):
        block = lax.dynamic_slice_in_dim(tensor, start, STEP_ROWS, 0)
        inner_sum = jnp.einsum("ikj,jr->ikr", block, run_bins_low, preferred_element_type=F32)
        row_terms = jnp.einsum("kr,ikr->ir", times, inner_sum, precision=HIGH)
        return lax.dynamic_update_slice_in_dim(total, row_terms, start, 0)

    local = sweep(step, jnp.zeros((rowcap, bins.shape[1]), F32))
    run_terms = lax.psum(local, "tm")
    runs = runs * run_terms / (jnp.dot(runs, bin_gram * time_gram, precision=HIGH) + 1.0 - live)
    return (runs, bins, times)


def split(x):
    hi = x.astype(BF16)
    return hi, (x - hi.astype(F32)).astype(BF16)


def dot_low(a, b):
    return lax.dot_general(a, b, (((1,), (0,)), ((), ())), preferred_element_type=F32)


def fold(x):
    half = x.shape[1] // 2
    return x[:, :half] + x[:, half:]


def self_gram(x):
    both = jnp.concatenate(split(x), axis=1)
    product = fold(
        lax.dot_general(both, both, (((0,), (0,)), ((), ())), preferred_element_type=F32)
    )
    half = product.shape[0] // 2
    return product[:half] + product[half:]


def dot_f32(a, b):
    right = jnp.concatenate(split(b), axis=1)
    return fold(
        dot_low(jnp.concatenate(split(a), axis=1), jnp.concatenate([right, right], axis=0))
    )


QUAD = 4
VMEM_LIMIT = 64 * 2**20 - 2**16


def kernel(
    n, m, count_in, tensor_in, run_in, bin_in, time_in,
    run_out, bin_out, time_out,
    count_ref, slabs, run_ref, bin_ref, time_ref,
    wide, wide_in, flipped, terms, terms_in,
    bins_all, inner_sum, halves, parts, parts_in, times_all, times_flat,
    load_sem, wide_s, wide_r, half_s, half_r, fwd_s, fwd_r, part_s, part_r, row_s, row_r,
    term_s, term_r, bin_s, bin_r, pass_s, pass_r, out_sem,
):
    me = lax.axis_index("runs")
    tm = lax.axis_index("tm")
    rows = run_ref.shape[0]
    kk = time_ref.shape[0]
    jj, rank = bin_ref.shape
    block = jj // (n * m)
    half = rows // m
    span = jj // m
    flat = tm * n + me
    zs = n // QUAD
    strip = QUAD * block

    z = me // QUAD
    q = lax.rem(me, QUAD)
    steps = [(k, t) for k in list(range(1, zs)) + [0] for t in range(QUAD) if (k, t) != (0, 0)]

    def ahead(k, t):
        return lax.rem(z + k, zs) * QUAD + lax.rem(q + t, QUAD)

    def behind(k, t):
        return lax.rem(z - k + zs, zs) * QUAD + lax.rem(q - t + QUAD, QUAD)

    def copy(src, dst, send, recv, run_index, tm_index):
        made = pltpu.make_async_remote_copy(
            src_ref=src, dst_ref=dst, send_sem=send, recv_sem=recv,
            device_id=(run_index, tm_index), device_id_type=MESH,
        )
        made.start()
        return made

    loads = [
        pltpu.make_async_copy(src, dst, load_sem.at[index])
        for index, (src, dst) in enumerate((
            (tensor_in, slabs.at[0]), (bin_in, bin_ref), (count_in, count_ref),
            (run_in, run_ref), (time_in, time_ref),
        ))
    ]
    for made in loads:
        made.start()

    barrier = pltpu.get_barrier_semaphore()
    for off in range(1, n * m):
        peer = lax.rem(flat + off, n * m)
        pl.semaphore_signal(
            barrier, inc=1, device_id=(lax.rem(peer, n), peer // n), device_id_type=MESH
        )
    for made in loads:
        made.wait()

    live = (lax.broadcasted_iota(jnp.int32, (rows, rank), 0) < count_ref[0]).astype(F32)
    runs = run_ref[...] * live
    halves[flat] = jnp.where(tm == 0, runs[:half], runs[rows - half:])
    tensor = slabs[0]
    times = time_ref[...]
    inner = dot_low(tensor, bin_ref[...].astype(BF16)).reshape(rows, kk, rank)
    upper = inner[0] * runs[0:1]
    for i in range(1, rows):
        upper = upper + inner[i] * runs[i:i + 1]
    lower = dot_f32(times, self_gram(runs) * self_gram(bin_ref[...]))
    both = jnp.concatenate([upper, lower], axis=1)
    for k in range(kk):
        parts[k] = both[k:k + 1]

    pl.semaphore_wait(barrier, n * m - 1)

    part_copies = []
    for off in range(1, n):
        peer = lax.rem(me + off, n)
        part_copies.append(
            copy(parts.at[peer], parts_in.at[off], part_s.at[off], part_r.at[off], peer, tm)
        )
    wide[...] = tensor.astype(F32)
    wide_copies = []
    for off in range(1, m):
        peer = lax.rem(tm + off, m)
        wide_copies.append(
            copy(wide, wide_in.at[off], wide_s.at[off], wide_r.at[off], me, peer)
        )
    half_copies = []
    for off in range(1, n):
        peer = lax.rem(me + off, n)
        half_copies.append(
            copy(halves.at[flat], halves.at[flat], half_s.at[off], half_r.at[off], peer, tm)
        )

    start = pl.multiple_of(tm * span, span)
    flipped[:, : rows * kk] = wide[:, pl.ds(start, span)].T.astype(BF16)

    total = parts[me]
    for made, off in zip(part_copies, range(1, n)):
        made.wait_recv()
        total = total + parts_in[off]
    times_all[flat] = time_ref[pl.ds(me, 1), :] * total[:, :rank] / total[:, rank:]
    row_copies = []
    for off in range(1, n * m):
        peer = lax.rem(flat + off, n * m)
        row_copies.append(
            copy(
                times_all.at[flat], times_all.at[flat], row_s.at[off], row_r.at[off],
                lax.rem(peer, n), peer // n,
            )
        )
    for made in half_copies:
        made.wait_recv()
    fwd_copies = []
    mine = pl.ds(tm * n, n)
    for off in range(1, m):
        peer = lax.rem(tm + off, m)
        fwd_copies.append(
            copy(halves.at[mine], halves.at[mine], fwd_s.at[off], fwd_r.at[off], me, peer)
        )
    for off in range(1, m):
        wide_copies[off - 1].wait_recv()
        slabs[off] = wide_in[off].astype(BF16)
        flipped[:, off * rows * kk:(off + 1) * rows * kk] = (
            wide_in[off, :, pl.ds(start, span)].T.astype(BF16)
        )
    for made in row_copies:
        made.wait_recv()
    for k in range(n * m):
        times_flat[k:k + 1, :] = times_all[k]

    weights = []
    for off in range(m):
        index = lax.rem(tm + off, m)
        low = times_flat[pl.ds(pl.multiple_of(index * kk, kk), kk), :].astype(BF16).astype(F32)
        weights.extend(low * runs[i:i + 1] for i in range(rows))
    weight = jnp.concatenate(split(jnp.concatenate(weights, axis=0)), axis=1)
    term_copies = {}
    for k in list(range(1, zs)) + [0]:
        to_z = lax.rem(z + k, zs)
        piece = flipped[pl.ds(pl.multiple_of(to_z * strip, strip), strip), :]
        terms[pl.ds(to_z * QUAD, QUAD)] = fold(dot_low(piece, weight)).reshape(QUAD, block, rank)
        for t in range(QUAD):
            if (k, t) != (0, 0):
                peer = ahead(k, t)
                term_copies[k, t] = copy(
                    terms.at[peer], terms_in.at[k, t], term_s.at[k, t], term_r.at[k, t], peer, tm
                )
    for made in fwd_copies:
        made.wait_recv()
    run_gram = self_gram(halves[...].reshape(n * m * half, rank))
    time_gram = self_gram(times_flat[...])
    own = bin_ref[pl.ds(pl.multiple_of(flat * block, block), block), :]
    scale = own / dot_f32(own, run_gram * time_gram)
    total = terms[me]
    for k, t in steps:
        term_copies[k, t].wait_recv()
        total = total + terms_in[k, t]
    bins_all[flat] = scale * total

    bin_copies = {}
    for k, t in steps:
        bin_copies[k, t] = copy(
            bins_all.at[flat], bins_all.at[flat], bin_s.at[k, t], bin_r.at[k, t], ahead(k, t), tm
        )
    other = lax.rem(tm + 1, m)
    pass_copies = {}

    def hand_on(k):
        for t in range(QUAD):
            if (k, t) != (0, 0):
                bin_copies[k, t].wait_recv()
            slot = tm * n + behind(k, t)
            pass_copies[k, t] = copy(
                bins_all.at[slot], bins_all.at[slot], pass_s.at[k, t], pass_r.at[k, t], me, other
            )

    writes = []

    def use(k, bin_gram):
        from_z = lax.rem(z - k + zs, zs)
        for t in range(QUAD):
            pass_copies[k, t].wait_recv()
        pieces = []
        for core in range(m):
            mine = pl.ds(core * n + from_z * QUAD, QUAD)
            pieces.append(bins_all[mine].reshape(strip, rank))
            made = pltpu.make_async_copy(bins_all.at[mine], bin_out.at[mine], out_sem.at[k, core])
            made.start()
            writes.append(made)
        bins = jnp.concatenate(pieces, axis=0)
        bins_low = bins.astype(BF16)
        some = self_gram(bins)
        for off in range(m):
            slab = jnp.concatenate(
                [
                    slabs[off, :, pl.ds(pl.multiple_of(core * span + from_z * strip, strip), strip)]
                    for core in range(m)
                ],
                axis=1,
            )
            product = dot_low(slab, bins_low)
            inner_sum[off] = product if k == 0 else inner_sum[off] + product
        return some if bin_gram is None else bin_gram + some

    bin_gram = None
    hand_on(0)
    for k in range(1, zs):
        hand_on(k)
        bin_gram = use(k - 1, bin_gram)
    bin_gram = use(zs - 1, bin_gram)
    run_terms = None
    for off in range(m):
        index = lax.rem(tm + off, m)
        weight = times_flat[pl.ds(pl.multiple_of(index * kk, kk), kk), :]
        some = jnp.sum(inner_sum[off].reshape(rows, kk, rank) * weight[None], axis=1)
        run_terms = some if run_terms is None else run_terms + some
    run_out[...] = runs * run_terms / (dot_f32(runs, bin_gram * time_gram) + 1.0 - live)
    time_out[...] = times_flat[pl.ds(pl.multiple_of(tm * kk, kk), kk), :]

    for made in part_copies + wide_copies + half_copies + row_copies + fwd_copies:
        made.wait_send()
    for store in (term_copies, bin_copies, pass_copies):
        for made in store.values():
            made.wait_send()
    for made in writes:
        made.wait()


def hand_out(run_in, bin_in, time_in, run_out, bin_out, time_out, runs, bins, times, in_s, out_s):
    size = bins.shape[0] // QUAD
    moves = [(run_in, runs, run_out), (time_in, times, time_out)]
    for index in range(QUAD):
        mine = pl.ds(index * size, size)
        moves.append((bin_in.at[mine], bins.at[mine], bin_out.at[mine]))
    loads = [pltpu.make_async_copy(a, b, in_s.at[i]) for i, (a, b, _) in enumerate(moves)]
    stores = [pltpu.make_async_copy(b, c, out_s.at[i]) for i, (_, b, c) in enumerate(moves)]
    for made in loads:
        made.start()
    for load, store in zip(loads, stores):
        load.wait()
        store.start()
    for made in stores:
        made.wait()


def fused(n, m, tensor, run_counts, run_init, bin_init, time_init):
    rows, kk, jj = tensor.shape
    rank = bin_init.shape[1]
    block = jj // (n * m)
    half = rows // m
    zs = n // QUAD
    dma = pltpu.SemaphoreType.DMA
    vmem = pl.BlockSpec(memory_space=pltpu.VMEM)
    anywhere = pl.BlockSpec(memory_space=pl.ANY)
    shapes = (
        jax.ShapeDtypeStruct((rows, rank), F32),
        jax.ShapeDtypeStruct((n * m, block, rank), F32),
        jax.ShapeDtypeStruct((kk, rank), F32),
    )
    results = pl.pallas_call(
        functools.partial(kernel, n, m),
        out_shape=shapes,
        in_specs=[anywhere] * 5,
        out_specs=(vmem, anywhere, vmem),
        scratch_shapes=[
            pltpu.SMEM((1,), jnp.int32),
            pltpu.VMEM((m, rows * kk, jj), BF16),
            pltpu.VMEM((rows, rank), F32),
            pltpu.VMEM((jj, rank), F32),
            pltpu.VMEM((kk, rank), F32),
            pltpu.VMEM((rows * kk, jj), F32),
            pltpu.VMEM((m, rows * kk, jj), F32),
            pltpu.VMEM((jj // m, m * rows * kk), BF16),
            pltpu.VMEM((n, block, rank), F32),
            pltpu.VMEM((zs, QUAD, block, rank), F32),
            pltpu.VMEM((n * m, block, rank), F32),
            pltpu.VMEM((m, rows * kk, rank), F32),
            pltpu.VMEM((n * m, half, rank), F32),
            pltpu.VMEM((n, 1, 2 * rank), F32),
            pltpu.VMEM((n, 1, 2 * rank), F32),
            pltpu.VMEM((n * m, 1, rank), F32),
            pltpu.VMEM((n * m, rank), F32),
            dma((5,)), dma((m,)), dma((m,)), dma((n,)), dma((n,)), dma((m,)), dma((m,)),
            dma((n,)), dma((n,)), dma((n * m,)), dma((n * m,)),
            dma((zs, QUAD)), dma((zs, QUAD)), dma((zs, QUAD)), dma((zs, QUAD)),
            dma((zs, QUAD)), dma((zs, QUAD)), dma((zs, m)),
        ],
        compiler_params=pltpu.CompilerParams(
            collective_id=0, has_side_effects=True, vmem_limit_bytes=VMEM_LIMIT
        ),
    )(run_counts, tensor.reshape(rows * kk, jj), run_init, bin_init, time_init)
    runs, bins, times = pl.pallas_call(
        hand_out,
        out_shape=shapes,
        in_specs=[anywhere] * 3,
        out_specs=[anywhere] * 3,
        scratch_shapes=[pltpu.VMEM(x.shape, F32) for x in shapes] + [dma((2 + QUAD,))] * 2,
        compiler_params=pltpu.CompilerParams(vmem_limit_bytes=VMEM_LIMIT),
    )(*results)
    return runs, bins.reshape(jj, rank), times


def update(n, m, *args):
    rows, kk, jj = args[0].shape
    fits = m == 2 and kk == n and n % QUAD == 0 and kk % 16 == 0 and rows % (8 * m) == 0
    fits = fits and jj % (8 * n * m) == 0 and (QUAD * jj // (n * m)) % 128 == 0
    return fused(n, m, *args) if fits else shards(*args)


def solution(mesh):
    return jax.shard_map(
        functools.partial(update, mesh.shape["runs"], mesh.shape["tm"]),
        mesh=mesh,
        in_specs=(P("runs", "tm", None), P("runs"), P("runs", None), P(), P("tm", None)),
        out_specs=(P("runs", None), P(), P("tm", None)),
        check_vma=False,
    )
```

```python
import functools

import jax
import jax.numpy as jnp
from jax import lax
from jax.experimental import pallas as pl
from jax.experimental.pallas import tpu as pltpu
from jax.sharding import PartitionSpec as P

HIGH = lax.Precision.HIGHEST
STEP_ROWS = 8
MESH = pl.DeviceIdType.MESH
F32 = jnp.float32
BF16 = jnp.bfloat16


def gram(factor):
    return jnp.dot(factor.T, factor, precision=HIGH)


def run_gram_sum(runs):
    return lax.psum(gram(runs), "runs")


def time_gram_sum(times):
    return lax.psum(gram(times), "tm")


def shards(tensor, run_counts, run_init, bin_init, time_init):
    rowcap = tensor.shape[0]
    count = run_counts[0]
    live = (jnp.arange(rowcap, dtype=jnp.int32) < count).astype(F32)[:, None]
    blocks = (count + STEP_ROWS - 1) // STEP_ROWS
    runs = run_init * live
    bins = bin_init
    times = time_init

    def sweep(step, init):
        return lax.fori_loop(0, blocks, lambda index, carry: step(index * STEP_ROWS, carry), init)

    run_gram = run_gram_sum(runs)
    bin_gram = gram(bins)
    bins_low = bins.astype(BF16)

    def step(start, total):
        block = lax.dynamic_slice_in_dim(tensor, start, STEP_ROWS, 0)
        rows = lax.dynamic_slice_in_dim(runs, start, STEP_ROWS, 0)
        inner_sum = jnp.einsum("ikj,jr->ikr", block, bins_low, preferred_element_type=F32)
        return total + jnp.einsum("ir,ikr->kr", rows, inner_sum, precision=HIGH)

    local = sweep(step, jnp.zeros((tensor.shape[1], bins.shape[1]), F32))
    time_terms = lax.psum(local, "runs")
    times = times * time_terms / jnp.dot(times, run_gram * bin_gram, precision=HIGH)
    time_gram = time_gram_sum(times)
    times_low = times.astype(BF16)

    def step(start, total):
        block = lax.dynamic_slice_in_dim(tensor, start, STEP_ROWS, 0)
        rows = lax.dynamic_slice_in_dim(runs, start, STEP_ROWS, 0)
        partial_value = jnp.einsum("ikj,kr->ijr", block, times_low, preferred_element_type=F32)
        return total + jnp.einsum("ir,ijr->jr", rows, partial_value, precision=HIGH)

    local_terms = sweep(step, jnp.zeros((tensor.shape[2], times.shape[1]), F32))
    mixing = run_gram * time_gram
    bin_terms = lax.psum(local_terms, ("runs", "tm"))
    bins = bins * bin_terms / jnp.dot(bins, mixing, precision=HIGH)
    bin_gram = gram(bins)
    run_bins_low = bins.astype(BF16)

    def step(start, total):
        block = lax.dynamic_slice_in_dim(tensor, start, STEP_ROWS, 0)
        inner_sum = jnp.einsum("ikj,jr->ikr", block, run_bins_low, preferred_element_type=F32)
        row_terms = jnp.einsum("kr,ikr->ir", times, inner_sum, precision=HIGH)
        return lax.dynamic_update_slice_in_dim(total, row_terms, start, 0)

    local = sweep(step, jnp.zeros((rowcap, bins.shape[1]), F32))
    run_terms = lax.psum(local, "tm")
    runs = runs * run_terms / (jnp.dot(runs, bin_gram * time_gram, precision=HIGH) + 1.0 - live)
    return (runs, bins, times)


def split(x):
    hi = x.astype(BF16)
    return hi, (x - hi.astype(F32)).astype(BF16)


def dot_low(a, b):
    return lax.dot_general(a, b, (((1,), (0,)), ((), ())), preferred_element_type=F32)


def fold(x):
    half = x.shape[1] // 2
    return x[:, :half] + x[:, half:]


def self_gram(x):
    both = jnp.concatenate(split(x), axis=1)
    product = fold(
        lax.dot_general(both, both, (((0,), (0,)), ((), ())), preferred_element_type=F32)
    )
    half = product.shape[0] // 2
    return product[:half] + product[half:]


def dot_f32(a, b):
    right = jnp.concatenate(split(b), axis=1)
    return fold(
        dot_low(jnp.concatenate(split(a), axis=1), jnp.concatenate([right, right], axis=0))
    )


QUAD = 4
VMEM_LIMIT = 64 * 2**20 - 2**16


def kernel(
    n, m, count_in, tensor_in, run_in, bin_in, time_in,
    run_out, bin_out, time_out,
    count_ref, slabs, run_ref, bin_ref, time_ref,
    wide, wide_in, flipped, terms, terms_in,
    bins_all, inner_sum, gram_sum, halves, parts, parts_in, times_all, times_flat,
    load_sem, wide_s, wide_r, half_s, half_r, fwd_s, fwd_r, part_s, part_r, row_s, row_r,
    term_s, term_r, bin_s, bin_r, pass_s, pass_r, out_sem,
):
    me = lax.axis_index("runs")
    tm = lax.axis_index("tm")
    rows = run_ref.shape[0]
    kk = time_ref.shape[0]
    jj, rank = bin_ref.shape
    block = jj // (n * m)
    half = rows // m
    span = jj // m
    flat = tm * n + me
    zs = n // QUAD
    strip = QUAD * block
    other = 1 - tm
    z = me // QUAD
    q = lax.rem(me, QUAD)

    def ahead(index):
        return lax.rem(z + index // QUAD, zs) * QUAD + lax.rem(q + index, QUAD)

    def move(src, dst, send, recv, run_index, tm_index):
        return pltpu.make_async_remote_copy(
            src_ref=src, dst_ref=dst, send_sem=send, recv_sem=recv,
            device_id=(run_index, tm_index), device_id_type=MESH,
        )

    def all_of(ref, send, recv):
        return move(ref, ref, send, recv, me, other)

    def loop(low, high, body):
        lax.fori_loop(low, high, lambda i, c: (body(i), c)[1], 0)

    def aligned(value, unit):
        return pl.ds(pl.multiple_of(value * unit, unit), unit)

    loads = [
        pltpu.make_async_copy(src, dst, load_sem.at[index])
        for index, (src, dst) in enumerate((
            (tensor_in, slabs.at[0]), (bin_in, bin_ref), (count_in, count_ref),
            (run_in, run_ref), (time_in, time_ref),
        ))
    ]
    for made in loads:
        made.start()

    barrier = pltpu.get_barrier_semaphore()

    def greet(off):
        peer = lax.rem(flat + off, n * m)
        pl.semaphore_signal(
            barrier, inc=1, device_id=(lax.rem(peer, n), peer // n), device_id_type=MESH
        )

    loop(1, n * m, greet)
    for made in loads:
        made.wait()

    live = (lax.broadcasted_iota(jnp.int32, (rows, rank), 0) < count_ref[0]).astype(F32)
    runs = run_ref[...] * live
    halves[flat] = jnp.where(tm == 0, runs[:half], runs[rows - half:])
    inner = dot_low(slabs[0], bin_ref[...].astype(BF16)).reshape(rows, kk, rank)
    upper = inner[0] * runs[0:1]
    for i in range(1, rows):
        upper = upper + inner[i] * runs[i:i + 1]
    gram_sum[...] = jnp.zeros_like(gram_sum)

    def gram_step(i):
        gram_sum[...] += self_gram(bin_ref[aligned(i, jj // zs), :])

    loop(0, zs, gram_step)
    lower = dot_f32(time_ref[...], self_gram(runs) * gram_sum[...])
    both = jnp.concatenate([upper, lower], axis=1)
    for k in range(kk):
        parts[k] = both[k:k + 1]

    pl.semaphore_wait(barrier, n * m - 1)

    def send_part(off):
        peer = lax.rem(me + off, n)
        move(parts.at[peer], parts_in.at[off], part_s, part_r, peer, tm).start()

    loop(1, n, send_part)

    chunk = rows * kk // 8

    def widen(i):
        wide[aligned(i, chunk), :] = slabs[0, aligned(i, chunk), :].astype(F32)

    loop(0, 8, widen)
    wide_copy = move(wide, wide_in, wide_s, wide_r, me, other)
    wide_copy.start()

    def send_half(off):
        peer = lax.rem(me + off, n)
        move(halves.at[flat], halves.at[flat], half_s, half_r, peer, tm).start()

    loop(1, n, send_half)

    def flip(source, place):
        def step(i):
            columns = aligned(tm * (span // strip) + i, strip)
            flipped[aligned(i, strip), place * rows * kk:(place + 1) * rows * kk] = (
                source[:, columns].T.astype(BF16)
            )

        loop(0, span // strip, step)

    flip(wide, 0)

    others = pl.ds(1, n - 1)
    all_of(parts_in.at[others], part_s, part_r).wait_recv()
    total = parts[me]
    for off in range(1, n):
        total = total + parts_in[off]
    times_all[flat] = time_ref[pl.ds(me, 1), :] * total[:, :rank] / total[:, rank:]

    def send_row(off):
        peer = lax.rem(flat + off, n * m)
        move(
            times_all.at[flat], times_all.at[flat], row_s, row_r, lax.rem(peer, n), peer // n
        ).start()

    loop(1, n * m, send_row)
    all_of(halves.at[others], half_s, half_r).wait_recv()
    mine = pl.ds(tm * n, n)
    fwd_copy = move(halves.at[mine], halves.at[mine], fwd_s, fwd_r, me, other)
    fwd_copy.start()
    wide_copy.wait_recv()
    flip(wide_in, 1)

    def narrow(i):
        slabs[1, aligned(i, chunk), :] = wide_in[aligned(i, chunk), :].astype(BF16)

    loop(0, 8, narrow)
    all_of(parts_in.at[others], part_s, part_r).wait_send()
    all_of(halves.at[others], half_s, half_r).wait_send()
    wide_copy.wait_send()
    all_of(times_all.at[pl.ds(1, n * m - 1)], row_s, row_r).wait_recv()
    for k in range(n * m):
        times_flat[k:k + 1, :] = times_all[k]

    weights = []
    for index in (tm, other):
        low = times_flat[aligned(index, kk), :].astype(BF16).astype(F32)
        weights.extend(low * runs[i:i + 1] for i in range(rows))
    weight = jnp.concatenate(split(jnp.concatenate(weights, axis=0)), axis=1)

    def send_term(index):
        peer = ahead(index)
        move(terms.at[peer], terms_in.at[index], term_s, term_r, peer, tm).start()

    for k in list(range(1, zs)) + [0]:
        to_z = lax.rem(z + k, zs)
        piece = flipped[aligned(to_z, strip), :]
        terms[pl.ds(to_z * QUAD, QUAD)] = fold(dot_low(piece, weight)).reshape(QUAD, block, rank)
        loop(max(k * QUAD, 1), (k + 1) * QUAD, send_term)
    all_of(times_all.at[pl.ds(1, n * m - 1)], row_s, row_r).wait_send()
    fwd_copy.wait()
    run_gram = self_gram(halves[...].reshape(n * m * half, rank))
    time_gram = self_gram(times_flat[...])
    own = bin_ref[aligned(flat, block), :]
    scale = own / dot_f32(own, run_gram * time_gram)
    gram_sum[...] = jnp.zeros_like(gram_sum)
    inner_sum[...] = jnp.zeros_like(inner_sum)
    total = terms[me]
    all_of(terms_in.at[others], term_s, term_r).wait_recv()
    for index in range(1, n):
        total = total + terms_in[index]
    bins_all[flat] = scale * total

    def send_bins(index):
        move(
            bins_all.at[flat], bins_all.at[flat], bin_s, bin_r.at[index // QUAD], ahead(index), tm
        ).start()

    loop(1, n, send_bins)
    all_of(terms_in.at[others], term_s, term_r).wait_send()

    def group(core, k):
        return pl.ds(core * n + lax.rem(z - k + zs, zs) * QUAD, QUAD)

    def hand_on(k):
        mine = bins_all.at[group(tm, k)]
        move(mine, mine, pass_s, pass_r.at[k], me, other).start()

    all_of(bins_all.at[pl.ds(0, QUAD - 1)], bin_s, bin_r.at[0]).wait_recv()
    hand_on(0)

    def arrive(k):
        all_of(bins_all.at[group(tm, k)], bin_s, bin_r.at[k]).wait_recv()
        hand_on(k)

    loop(1, zs, arrive)

    def use(k):
        from_z = lax.rem(z - k + zs, zs)
        all_of(bins_all.at[group(other, k)], pass_s, pass_r.at[k]).wait_recv()
        pieces = []
        for core in range(m):
            mine = group(core, k)
            pieces.append(bins_all[mine].reshape(strip, rank))
            pltpu.make_async_copy(bins_all.at[mine], bin_out.at[mine], out_sem.at[k, core]).start()
        bins = jnp.concatenate(pieces, axis=0)
        bins_low = bins.astype(BF16)
        gram_sum[...] += self_gram(bins)
        for off in range(m):
            slab = jnp.concatenate(
                [slabs[off, :, aligned(core * zs + from_z, strip)] for core in range(m)], axis=1
            )
            inner_sum[off] += dot_low(slab, bins_low)

    loop(0, zs, use)
    run_terms = None
    for off, index in enumerate((tm, other)):
        weight = times_flat[aligned(index, kk), :]
        some = jnp.sum(inner_sum[off].reshape(rows, kk, rank) * weight[None], axis=1)
        run_terms = some if run_terms is None else run_terms + some
    run_out[...] = runs * run_terms / (dot_f32(runs, gram_sum[...] * time_gram) + 1.0 - live)
    time_out[...] = times_flat[aligned(tm, kk), :]
    all_of(bins_all.at[others], bin_s, bin_r.at[0]).wait_send()
    all_of(bins_all.at[mine], pass_s, pass_r.at[0]).wait_send()

    def finish(k):
        for core in range(m):
            mine = group(core, k)
            pltpu.make_async_copy(bins_all.at[mine], bin_out.at[mine], out_sem.at[k, core]).wait()

    loop(0, zs, finish)


def hand_out(run_in, bin_in, time_in, run_out, bin_out, time_out, runs, bins, times, in_s, out_s):
    size = bins.shape[0] // QUAD
    moves = [(run_in, runs, run_out), (time_in, times, time_out)]
    for index in range(QUAD):
        mine = pl.ds(index * size, size)
        moves.append((bin_in.at[mine], bins.at[mine], bin_out.at[mine]))
    loads = [pltpu.make_async_copy(a, b, in_s.at[i]) for i, (a, b, _) in enumerate(moves)]
    stores = [pltpu.make_async_copy(b, c, out_s.at[i]) for i, (_, b, c) in enumerate(moves)]
    for made in loads:
        made.start()
    for load, store in zip(loads, stores):
        load.wait()
        store.start()
    for made in stores:
        made.wait()


def fused(n, m, tensor, run_counts, run_init, bin_init, time_init):
    rows, kk, jj = tensor.shape
    rank = bin_init.shape[1]
    block = jj // (n * m)
    half = rows // m
    zs = n // QUAD
    dma = pltpu.SemaphoreType.DMA
    vmem = pl.BlockSpec(memory_space=pltpu.VMEM)
    anywhere = pl.BlockSpec(memory_space=pl.ANY)
    shapes = (
        jax.ShapeDtypeStruct((rows, rank), F32),
        jax.ShapeDtypeStruct((n * m, block, rank), F32),
        jax.ShapeDtypeStruct((kk, rank), F32),
    )
    results = pl.pallas_call(
        functools.partial(kernel, n, m),
        out_shape=shapes,
        in_specs=[anywhere] * 5,
        out_specs=(vmem, anywhere, vmem),
        scratch_shapes=[
            pltpu.SMEM((1,), jnp.int32),
            pltpu.VMEM((m, rows * kk, jj), BF16),
            pltpu.VMEM((rows, rank), F32),
            pltpu.VMEM((jj, rank), F32),
            pltpu.VMEM((kk, rank), F32),
            pltpu.VMEM((rows * kk, jj), F32),
            pltpu.VMEM((rows * kk, jj), F32),
            pltpu.VMEM((jj // m, m * rows * kk), BF16),
            pltpu.VMEM((n, block, rank), F32),
            pltpu.VMEM((n, block, rank), F32),
            pltpu.VMEM((n * m, block, rank), F32),
            pltpu.VMEM((m, rows * kk, rank), F32),
            pltpu.VMEM((rank, rank), F32),
            pltpu.VMEM((n * m, half, rank), F32),
            pltpu.VMEM((n, 1, 2 * rank), F32),
            pltpu.VMEM((n, 1, 2 * rank), F32),
            pltpu.VMEM((n * m, 1, rank), F32),
            pltpu.VMEM((n * m, rank), F32),
            dma((5,)), *[dma] * 12, dma, dma((zs,)), dma, dma((zs,)), dma((zs, m)),
        ],
        compiler_params=pltpu.CompilerParams(
            collective_id=0, has_side_effects=True, vmem_limit_bytes=VMEM_LIMIT
        ),
    )(run_counts, tensor.reshape(rows * kk, jj), run_init, bin_init, time_init)
    runs, bins, times = pl.pallas_call(
        hand_out,
        out_shape=shapes,
        in_specs=[anywhere] * 3,
        out_specs=[anywhere] * 3,
        scratch_shapes=[pltpu.VMEM(x.shape, F32) for x in shapes] + [dma((2 + QUAD,))] * 2,
        compiler_params=pltpu.CompilerParams(vmem_limit_bytes=VMEM_LIMIT),
    )(*results)
    return runs, bins.reshape(jj, rank), times


def update(n, m, *args):
    rows, kk, jj = args[0].shape
    fits = m == 2 and kk == n and n % QUAD == 0 and kk % 16 == 0 and rows % (8 * m) == 0
    fits = fits and jj % (8 * n * m) == 0 and (QUAD * jj // (n * m)) % 128 == 0
    return fused(n, m, *args) if fits else shards(*args)


def solution(mesh):
    return jax.shard_map(
        functools.partial(update, mesh.shape["runs"], mesh.shape["tm"]),
        mesh=mesh,
        in_specs=(P("runs", "tm", None), P("runs"), P("runs", None), P(), P("tm", None)),
        out_specs=(P("runs", None), P(), P("tm", None)),
        check_vma=False,
    )
```

```python
import functools

import jax
import jax.numpy as jnp
from jax import lax
from jax.experimental import pallas as pl
from jax.experimental.pallas import tpu as pltpu
from jax.sharding import PartitionSpec as P

HIGH = lax.Precision.HIGHEST
STEP_ROWS = 8
MESH = pl.DeviceIdType.MESH
F32 = jnp.float32
BF16 = jnp.bfloat16


def gram(factor):
    return jnp.dot(factor.T, factor, precision=HIGH)


def run_gram_sum(runs):
    return lax.psum(gram(runs), "runs")


def time_gram_sum(times):
    return lax.psum(gram(times), "tm")


def shards(tensor, run_counts, run_init, bin_init, time_init):
    rowcap = tensor.shape[0]
    count = run_counts[0]
    live = (jnp.arange(rowcap, dtype=jnp.int32) < count).astype(F32)[:, None]
    blocks = (count + STEP_ROWS - 1) // STEP_ROWS
    runs = run_init * live
    bins = bin_init
    times = time_init

    def sweep(step, init):
        return lax.fori_loop(0, blocks, lambda index, carry: step(index * STEP_ROWS, carry), init)

    run_gram = run_gram_sum(runs)
    bin_gram = gram(bins)
    bins_low = bins.astype(BF16)

    def step(start, total):
        block = lax.dynamic_slice_in_dim(tensor, start, STEP_ROWS, 0)
        rows = lax.dynamic_slice_in_dim(runs, start, STEP_ROWS, 0)
        inner_sum = jnp.einsum("ikj,jr->ikr", block, bins_low, preferred_element_type=F32)
        return total + jnp.einsum("ir,ikr->kr", rows, inner_sum, precision=HIGH)

    local = sweep(step, jnp.zeros((tensor.shape[1], bins.shape[1]), F32))
    time_terms = lax.psum(local, "runs")
    times = times * time_terms / jnp.dot(times, run_gram * bin_gram, precision=HIGH)
    time_gram = time_gram_sum(times)
    times_low = times.astype(BF16)

    def step(start, total):
        block = lax.dynamic_slice_in_dim(tensor, start, STEP_ROWS, 0)
        rows = lax.dynamic_slice_in_dim(runs, start, STEP_ROWS, 0)
        partial_value = jnp.einsum("ikj,kr->ijr", block, times_low, preferred_element_type=F32)
        return total + jnp.einsum("ir,ijr->jr", rows, partial_value, precision=HIGH)

    local_terms = sweep(step, jnp.zeros((tensor.shape[2], times.shape[1]), F32))
    mixing = run_gram * time_gram
    bin_terms = lax.psum(local_terms, ("runs", "tm"))
    bins = bins * bin_terms / jnp.dot(bins, mixing, precision=HIGH)
    bin_gram = gram(bins)
    run_bins_low = bins.astype(BF16)

    def step(start, total):
        block = lax.dynamic_slice_in_dim(tensor, start, STEP_ROWS, 0)
        inner_sum = jnp.einsum("ikj,jr->ikr", block, run_bins_low, preferred_element_type=F32)
        row_terms = jnp.einsum("kr,ikr->ir", times, inner_sum, precision=HIGH)
        return lax.dynamic_update_slice_in_dim(total, row_terms, start, 0)

    local = sweep(step, jnp.zeros((rowcap, bins.shape[1]), F32))
    run_terms = lax.psum(local, "tm")
    runs = runs * run_terms / (jnp.dot(runs, bin_gram * time_gram, precision=HIGH) + 1.0 - live)
    return (runs, bins, times)


def split(x):
    hi = x.astype(BF16)
    return hi, (x - hi.astype(F32)).astype(BF16)


def dot_low(a, b):
    return lax.dot_general(a, b, (((1,), (0,)), ((), ())), preferred_element_type=F32)


def fold(x):
    half = x.shape[1] // 2
    return x[:, :half] + x[:, half:]


def self_gram(x):
    both = jnp.concatenate(split(x), axis=1)
    product = fold(
        lax.dot_general(both, both, (((0,), (0,)), ((), ())), preferred_element_type=F32)
    )
    half = product.shape[0] // 2
    return product[:half] + product[half:]


def dot_f32(a, b):
    right = jnp.concatenate(split(b), axis=1)
    return fold(
        dot_low(jnp.concatenate(split(a), axis=1), jnp.concatenate([right, right], axis=0))
    )


QUAD = 4
VMEM_LIMIT = 64 * 2**20 - 2**16


def kernel(
    n, m, count_in, tensor_in, run_in, bin_in, time_in,
    run_out, bin_out, time_out,
    count_ref, slabs, run_ref, bin_ref, time_ref,
    wide, wide_in, flipped, terms, terms_in,
    bins_all, inner_sum, gram_sum, halves, parts, parts_in, times_all, times_flat,
    load_sem, wide_s, wide_r, half_s, half_r, fwd_s, fwd_r, part_s, part_r, row_s, row_r,
    term_s, term_r, bin_s, bin_r, along_r, pass_s, pass_r, out_sem,
):
    me = lax.axis_index("runs")
    tm = lax.axis_index("tm")
    rows = run_ref.shape[0]
    kk = time_ref.shape[0]
    jj, rank = bin_ref.shape
    block = jj // (n * m)
    half = rows // m
    span = jj // m
    flat = tm * n + me
    zs = n // QUAD
    strip = QUAD * block
    other = 1 - tm
    z = me // QUAD
    q = lax.rem(me, QUAD)

    def ahead(index):
        return lax.rem(z + index // QUAD, zs) * QUAD + lax.rem(q + index, QUAD)

    def move(src, dst, send, recv, run_index, tm_index):
        return pltpu.make_async_remote_copy(
            src_ref=src, dst_ref=dst, send_sem=send, recv_sem=recv,
            device_id=(run_index, tm_index), device_id_type=MESH,
        )

    def all_of(ref, send, recv):
        return move(ref, ref, send, recv, me, other)

    def loop(low, high, body):
        lax.fori_loop(low, high, lambda i, c: (body(i), c)[1], 0)

    def aligned(value, unit):
        return pl.ds(pl.multiple_of(value * unit, unit), unit)

    loads = [
        pltpu.make_async_copy(src, dst, load_sem.at[index])
        for index, (src, dst) in enumerate((
            (tensor_in, slabs.at[0]), (bin_in, bin_ref), (count_in, count_ref),
            (run_in, run_ref), (time_in, time_ref),
        ))
    ]
    for made in loads:
        made.start()

    barrier = pltpu.get_barrier_semaphore()

    def greet(off):
        peer = lax.rem(flat + off, n * m)
        pl.semaphore_signal(
            barrier, inc=1, device_id=(lax.rem(peer, n), peer // n), device_id_type=MESH
        )

    loop(1, n * m, greet)
    for made in loads:
        made.wait()

    live = (lax.broadcasted_iota(jnp.int32, (rows, rank), 0) < count_ref[0]).astype(F32)
    runs = run_ref[...] * live
    halves[flat] = jnp.where(tm == 0, runs[:half], runs[rows - half:])
    inner = dot_low(slabs[0], bin_ref[...].astype(BF16)).reshape(rows, kk, rank)
    upper = inner[0] * runs[0:1]
    for i in range(1, rows):
        upper = upper + inner[i] * runs[i:i + 1]
    gram_sum[...] = jnp.zeros_like(gram_sum)

    def gram_step(i):
        gram_sum[...] += self_gram(bin_ref[aligned(i, jj // zs), :])

    loop(0, zs, gram_step)
    lower = dot_f32(time_ref[...], self_gram(runs) * gram_sum[...])
    both = jnp.concatenate([upper, lower], axis=1)
    for k in range(kk):
        parts[k] = both[k:k + 1]

    pl.semaphore_wait(barrier, n * m - 1)

    def send_part(off):
        peer = lax.rem(me + off, n)
        move(parts.at[peer], parts_in.at[off], part_s, part_r, peer, tm).start()

    loop(1, n, send_part)

    chunk = rows * kk // 8

    def widen(i):
        wide[aligned(i, chunk), :] = slabs[0, aligned(i, chunk), :].astype(F32)

    loop(0, 8, widen)
    wide_copy = move(wide, wide_in, wide_s, wide_r, me, other)
    wide_copy.start()

    def send_half(off):
        peer = lax.rem(me + off, n)
        move(halves.at[flat], halves.at[flat], half_s, half_r, peer, tm).start()

    loop(1, n, send_half)

    def flip(source, place):
        def step(i):
            columns = aligned(tm * (span // strip) + i, strip)
            flipped[aligned(i, strip), place * rows * kk:(place + 1) * rows * kk] = (
                source[:, columns].T.astype(BF16)
            )

        loop(0, span // strip, step)

    flip(wide, 0)

    others = pl.ds(1, n - 1)
    all_of(parts_in.at[others], part_s, part_r).wait_recv()
    total = parts[me]
    for off in range(1, n):
        total = total + parts_in[off]
    times_all[flat] = time_ref[pl.ds(me, 1), :] * total[:, :rank] / total[:, rank:]

    def send_row(off):
        peer = lax.rem(flat + off, n * m)
        move(
            times_all.at[flat], times_all.at[flat], row_s, row_r, lax.rem(peer, n), peer // n
        ).start()

    loop(1, n * m, send_row)
    all_of(halves.at[others], half_s, half_r).wait_recv()
    mine = pl.ds(tm * n, n)
    fwd_copy = move(halves.at[mine], halves.at[mine], fwd_s, fwd_r, me, other)
    fwd_copy.start()
    wide_copy.wait_recv()
    flip(wide_in, 1)

    def narrow(i):
        slabs[1, aligned(i, chunk), :] = wide_in[aligned(i, chunk), :].astype(BF16)

    loop(0, 8, narrow)
    all_of(parts_in.at[others], part_s, part_r).wait_send()
    all_of(halves.at[others], half_s, half_r).wait_send()
    wide_copy.wait_send()
    all_of(times_all.at[pl.ds(1, n * m - 1)], row_s, row_r).wait_recv()
    for k in range(n * m):
        times_flat[k:k + 1, :] = times_all[k]

    weights = []
    for index in (tm, other):
        low = times_flat[aligned(index, kk), :].astype(BF16).astype(F32)
        weights.extend(low * runs[i:i + 1] for i in range(rows))
    weight = jnp.concatenate(split(jnp.concatenate(weights, axis=0)), axis=1)

    def send_term(index):
        peer = ahead(index)
        move(terms.at[peer], terms_in.at[index], term_s, term_r, peer, tm).start()

    for k in list(range(1, zs)) + [0]:
        to_z = lax.rem(z + k, zs)
        piece = flipped[aligned(to_z, strip), :]
        terms[pl.ds(to_z * QUAD, QUAD)] = fold(dot_low(piece, weight)).reshape(QUAD, block, rank)
        loop(max(k * QUAD, 1), (k + 1) * QUAD, send_term)
    all_of(times_all.at[pl.ds(1, n * m - 1)], row_s, row_r).wait_send()
    fwd_copy.wait()
    run_gram = self_gram(halves[...].reshape(n * m * half, rank))
    time_gram = self_gram(times_flat[...])
    own = bin_ref[aligned(flat, block), :]
    scale = own / dot_f32(own, run_gram * time_gram)
    gram_sum[...] = jnp.zeros_like(gram_sum)
    inner_sum[...] = jnp.zeros_like(inner_sum)
    total = terms[me]
    all_of(terms_in.at[others], term_s, term_r).wait_recv()
    for index in range(1, n):
        total = total + terms_in[index]
    bins_all[flat] = scale * total

    def group(core, k):
        return pl.ds(core * n + lax.rem(z - k + zs, zs) * QUAD, QUAD)

    def send_along(k):
        mine = bins_all.at[flat]
        move(mine, mine, bin_s, along_r.at[k], ahead(k * QUAD), tm).start()

    def send_around(k):
        held = bins_all.at[tm * n + lax.rem(z - k + zs, zs) * QUAD + q]

        def step(t):
            move(held, held, bin_s, bin_r.at[k], ahead(t), tm).start()

        loop(1, QUAD, step)

    loop(1, zs, send_along)
    send_around(0)
    all_of(terms_in.at[others], term_s, term_r).wait_send()

    def relay(k):
        all_of(bins_all.at[0], bin_s, along_r.at[k]).wait_recv()
        send_around(k)

    loop(1, zs, relay)

    def hand_on(k):
        all_of(bins_all.at[pl.ds(0, QUAD - 1)], bin_s, bin_r.at[k]).wait_recv()
        mine = bins_all.at[group(tm, k)]
        move(mine, mine, pass_s, pass_r.at[k], me, other).start()

    loop(0, zs, hand_on)

    def use(k):
        from_z = lax.rem(z - k + zs, zs)
        all_of(bins_all.at[group(other, k)], pass_s, pass_r.at[k]).wait_recv()
        pieces = []
        for core in range(m):
            mine = group(core, k)
            pieces.append(bins_all[mine].reshape(strip, rank))
            pltpu.make_async_copy(bins_all.at[mine], bin_out.at[mine], out_sem.at[k, core]).start()
        bins = jnp.concatenate(pieces, axis=0)
        bins_low = bins.astype(BF16)
        gram_sum[...] += self_gram(bins)
        for off in range(m):
            slab = jnp.concatenate(
                [slabs[off, :, aligned(core * zs + from_z, strip)] for core in range(m)], axis=1
            )
            inner_sum[off] += dot_low(slab, bins_low)

    loop(0, zs, use)
    run_terms = None
    for off, index in enumerate((tm, other)):
        weight = times_flat[aligned(index, kk), :]
        some = jnp.sum(inner_sum[off].reshape(rows, kk, rank) * weight[None], axis=1)
        run_terms = some if run_terms is None else run_terms + some
    run_out[...] = runs * run_terms / (dot_f32(runs, gram_sum[...] * time_gram) + 1.0 - live)
    time_out[...] = times_flat[aligned(tm, kk), :]
    all_of(bins_all.at[others], bin_s, bin_r.at[0]).wait_send()
    all_of(bins_all.at[mine], pass_s, pass_r.at[0]).wait_send()

    def finish(k):
        for core in range(m):
            mine = group(core, k)
            pltpu.make_async_copy(bins_all.at[mine], bin_out.at[mine], out_sem.at[k, core]).wait()

    loop(0, zs, finish)


def hand_out(run_in, bin_in, time_in, run_out, bin_out, time_out, runs, bins, times, in_s, out_s):
    size = bins.shape[0] // QUAD
    moves = [(run_in, runs, run_out), (time_in, times, time_out)]
    for index in range(QUAD):
        mine = pl.ds(index * size, size)
        moves.append((bin_in.at[mine], bins.at[mine], bin_out.at[mine]))
    loads = [pltpu.make_async_copy(a, b, in_s.at[i]) for i, (a, b, _) in enumerate(moves)]
    stores = [pltpu.make_async_copy(b, c, out_s.at[i]) for i, (_, b, c) in enumerate(moves)]
    for made in loads:
        made.start()
    for load, store in zip(loads, stores):
        load.wait()
        store.start()
    for made in stores:
        made.wait()


def fused(n, m, tensor, run_counts, run_init, bin_init, time_init):
    rows, kk, jj = tensor.shape
    rank = bin_init.shape[1]
    block = jj // (n * m)
    half = rows // m
    zs = n // QUAD
    dma = pltpu.SemaphoreType.DMA
    vmem = pl.BlockSpec(memory_space=pltpu.VMEM)
    anywhere = pl.BlockSpec(memory_space=pl.ANY)
    shapes = (
        jax.ShapeDtypeStruct((rows, rank), F32),
        jax.ShapeDtypeStruct((n * m, block, rank), F32),
        jax.ShapeDtypeStruct((kk, rank), F32),
    )
    results = pl.pallas_call(
        functools.partial(kernel, n, m),
        out_shape=shapes,
        in_specs=[anywhere] * 5,
        out_specs=(vmem, anywhere, vmem),
        scratch_shapes=[
            pltpu.SMEM((1,), jnp.int32),
            pltpu.VMEM((m, rows * kk, jj), BF16),
            pltpu.VMEM((rows, rank), F32),
            pltpu.VMEM((jj, rank), F32),
            pltpu.VMEM((kk, rank), F32),
            pltpu.VMEM((rows * kk, jj), F32),
            pltpu.VMEM((rows * kk, jj), F32),
            pltpu.VMEM((jj // m, m * rows * kk), BF16),
            pltpu.VMEM((n, block, rank), F32),
            pltpu.VMEM((n, block, rank), F32),
            pltpu.VMEM((n * m, block, rank), F32),
            pltpu.VMEM((m, rows * kk, rank), F32),
            pltpu.VMEM((rank, rank), F32),
            pltpu.VMEM((n * m, half, rank), F32),
            pltpu.VMEM((n, 1, 2 * rank), F32),
            pltpu.VMEM((n, 1, 2 * rank), F32),
            pltpu.VMEM((n * m, 1, rank), F32),
            pltpu.VMEM((n * m, rank), F32),
            dma((5,)), *[dma] * 12, dma, dma((zs,)), dma((zs,)), dma, dma((zs,)), dma((zs, m)),
        ],
        compiler_params=pltpu.CompilerParams(
            collective_id=0, has_side_effects=True, vmem_limit_bytes=VMEM_LIMIT
        ),
    )(run_counts, tensor.reshape(rows * kk, jj), run_init, bin_init, time_init)
    runs, bins, times = pl.pallas_call(
        hand_out,
        out_shape=shapes,
        in_specs=[anywhere] * 3,
        out_specs=[anywhere] * 3,
        scratch_shapes=[pltpu.VMEM(x.shape, F32) for x in shapes] + [dma((2 + QUAD,))] * 2,
        compiler_params=pltpu.CompilerParams(vmem_limit_bytes=VMEM_LIMIT),
    )(*results)
    return runs, bins.reshape(jj, rank), times


def update(n, m, *args):
    rows, kk, jj = args[0].shape
    fits = m == 2 and kk == n and n % QUAD == 0 and kk % 16 == 0 and rows % (8 * m) == 0
    fits = fits and jj % (8 * n * m) == 0 and (QUAD * jj // (n * m)) % 128 == 0
    return fused(n, m, *args) if fits else shards(*args)


def solution(mesh):
    return jax.shard_map(
        functools.partial(update, mesh.shape["runs"], mesh.shape["tm"]),
        mesh=mesh,
        in_specs=(P("runs", "tm", None), P("runs"), P("runs", None), P(), P("tm", None)),
        out_specs=(P("runs", None), P(), P("tm", None)),
        check_vma=False,
    )
```

```python
import functools

import jax
import jax.numpy as jnp
from jax import lax
from jax.experimental import pallas as pl
from jax.experimental.pallas import tpu as pltpu
from jax.sharding import PartitionSpec as P

HIGH = lax.Precision.HIGHEST
STEP_ROWS = 8
MESH = pl.DeviceIdType.MESH
F32 = jnp.float32
BF16 = jnp.bfloat16


def gram(factor):
    return jnp.dot(factor.T, factor, precision=HIGH)


def run_gram_sum(runs):
    return lax.psum(gram(runs), "runs")


def time_gram_sum(times):
    return lax.psum(gram(times), "tm")


def shards(tensor, run_counts, run_init, bin_init, time_init):
    rowcap = tensor.shape[0]
    count = run_counts[0]
    live = (jnp.arange(rowcap, dtype=jnp.int32) < count).astype(F32)[:, None]
    blocks = (count + STEP_ROWS - 1) // STEP_ROWS
    runs = run_init * live
    bins = bin_init
    times = time_init

    def sweep(step, init):
        return lax.fori_loop(0, blocks, lambda index, carry: step(index * STEP_ROWS, carry), init)

    run_gram = run_gram_sum(runs)
    bin_gram = gram(bins)
    bins_low = bins.astype(BF16)

    def step(start, total):
        block = lax.dynamic_slice_in_dim(tensor, start, STEP_ROWS, 0)
        rows = lax.dynamic_slice_in_dim(runs, start, STEP_ROWS, 0)
        inner_sum = jnp.einsum("ikj,jr->ikr", block, bins_low, preferred_element_type=F32)
        return total + jnp.einsum("ir,ikr->kr", rows, inner_sum, precision=HIGH)

    local = sweep(step, jnp.zeros((tensor.shape[1], bins.shape[1]), F32))
    time_terms = lax.psum(local, "runs")
    times = times * time_terms / jnp.dot(times, run_gram * bin_gram, precision=HIGH)
    time_gram = time_gram_sum(times)
    times_low = times.astype(BF16)

    def step(start, total):
        block = lax.dynamic_slice_in_dim(tensor, start, STEP_ROWS, 0)
        rows = lax.dynamic_slice_in_dim(runs, start, STEP_ROWS, 0)
        partial_value = jnp.einsum("ikj,kr->ijr", block, times_low, preferred_element_type=F32)
        return total + jnp.einsum("ir,ijr->jr", rows, partial_value, precision=HIGH)

    local_terms = sweep(step, jnp.zeros((tensor.shape[2], times.shape[1]), F32))
    mixing = run_gram * time_gram
    bin_terms = lax.psum(local_terms, ("runs", "tm"))
    bins = bins * bin_terms / jnp.dot(bins, mixing, precision=HIGH)
    bin_gram = gram(bins)
    run_bins_low = bins.astype(BF16)

    def step(start, total):
        block = lax.dynamic_slice_in_dim(tensor, start, STEP_ROWS, 0)
        inner_sum = jnp.einsum("ikj,jr->ikr", block, run_bins_low, preferred_element_type=F32)
        row_terms = jnp.einsum("kr,ikr->ir", times, inner_sum, precision=HIGH)
        return lax.dynamic_update_slice_in_dim(total, row_terms, start, 0)

    local = sweep(step, jnp.zeros((rowcap, bins.shape[1]), F32))
    run_terms = lax.psum(local, "tm")
    runs = runs * run_terms / (jnp.dot(runs, bin_gram * time_gram, precision=HIGH) + 1.0 - live)
    return (runs, bins, times)


def split(x):
    hi = x.astype(BF16)
    return hi, (x - hi.astype(F32)).astype(BF16)


def dot_low(a, b):
    return lax.dot_general(a, b, (((1,), (0,)), ((), ())), preferred_element_type=F32)


def fold(x):
    half = x.shape[1] // 2
    return x[:, :half] + x[:, half:]


def self_gram(x):
    both = jnp.concatenate(split(x), axis=1)
    product = fold(
        lax.dot_general(both, both, (((0,), (0,)), ((), ())), preferred_element_type=F32)
    )
    half = product.shape[0] // 2
    return product[:half] + product[half:]


def dot_f32(a, b):
    right = jnp.concatenate(split(b), axis=1)
    return fold(
        dot_low(jnp.concatenate(split(a), axis=1), jnp.concatenate([right, right], axis=0))
    )


QUAD = 4
VMEM_LIMIT = 64 * 2**20 - 2**16


def kernel(
    n, m, count_in, tensor_in, run_in, bin_in, time_in,
    run_out, bin_out, time_out,
    count_ref, slabs, run_ref, bin_ref, time_ref,
    wide, wide_in, flipped, terms, terms_in,
    bins_all, inner_sum, runs_all, parts, parts_in, times_all, times_flat,
    load_sem, wide_s, wide_r, half_s, half_r, part_s, part_r, row_s, row_r,
    term_s, term_r, bin_s, bin_r, pass_s, pass_r, out_sem,
):
    me = lax.axis_index("runs")
    tm = lax.axis_index("tm")
    rows = run_ref.shape[0]
    kk = time_ref.shape[0]
    jj, rank = bin_ref.shape
    block = jj // (n * m)
    span = jj // m
    flat = tm * n + me
    zs = n // QUAD
    strip = QUAD * block
    other = 1 - tm
    z = me // QUAD
    q = lax.rem(me, QUAD)

    def ahead(index):
        return lax.rem(z + index // QUAD, zs) * QUAD + lax.rem(q + index, QUAD)

    def move(src, dst, send, recv, run_index, tm_index):
        return pltpu.make_async_remote_copy(
            src_ref=src, dst_ref=dst, send_sem=send, recv_sem=recv,
            device_id=(run_index, tm_index), device_id_type=MESH,
        )

    def all_of(ref, send, recv):
        return move(ref, ref, send, recv, me, other)

    def loop(low, high, body):
        lax.fori_loop(low, high, lambda i, c: (body(i), c)[1], 0)

    def aligned(value, unit):
        return pl.ds(pl.multiple_of(value * unit, unit), unit)

    loads = [
        pltpu.make_async_copy(src, dst, load_sem.at[index])
        for index, (src, dst) in enumerate((
            (tensor_in, slabs.at[0]), (bin_in, bin_ref), (count_in, count_ref),
            (run_in, run_ref), (time_in, time_ref),
        ))
    ]
    for made in loads:
        made.start()

    barrier = pltpu.get_barrier_semaphore()

    def greet(off):
        peer = lax.rem(flat + off, n * m)
        pl.semaphore_signal(
            barrier, inc=1, device_id=(lax.rem(peer, n), peer // n), device_id_type=MESH
        )

    loop(1, n * m, greet)
    for made in loads:
        made.wait()

    live = (lax.broadcasted_iota(jnp.int32, (rows, rank), 0) < count_ref[0]).astype(F32)
    runs = run_ref[...] * live
    runs_all[me] = runs
    inner = dot_low(slabs[0], bin_ref[...].astype(BF16)).reshape(rows, kk, rank)
    upper = inner[0] * runs[0:1]
    for i in range(1, rows):
        upper = upper + inner[i] * runs[i:i + 1]
    for k in range(kk):
        parts[k] = upper[k:k + 1]

    pl.semaphore_wait(barrier, n * m - 1)

    def send_part(off):
        peer = lax.rem(me + off, n)
        move(runs_all.at[me], runs_all.at[me], half_s, half_r, peer, tm).start()
        move(parts.at[peer], parts_in.at[off], part_s, part_r, peer, tm).start()

    loop(1, n, send_part)

    chunk = rows * kk // 8

    def widen(i):
        wide[aligned(i, chunk), :] = slabs[0, aligned(i, chunk), :].astype(F32)

    loop(0, 8, widen)
    wide_copy = move(wide, wide_in, wide_s, wide_r, me, other)
    wide_copy.start()

    bin_gram = self_gram(bin_ref[...])

    def flip(source, place):
        def step(i):
            columns = aligned(tm * (span // strip) + i, strip)
            flipped[aligned(i, strip), place * rows * kk:(place + 1) * rows * kk] = (
                source[:, columns].T.astype(BF16)
            )

        loop(0, span // strip, step)

    others = pl.ds(1, n - 1)
    all_of(runs_all.at[others], half_s, half_r).wait_recv()
    run_gram = self_gram(runs_all[...].reshape(n * rows, rank))
    lower = dot_f32(time_ref[...], run_gram * bin_gram)
    times_flat[pl.ds(0, kk), :] = time_ref[...] / lower
    ratio = times_flat[pl.ds(me, 1), :]
    all_of(parts_in.at[others], part_s, part_r).wait_recv()
    total = parts[me]
    for off in range(1, n):
        total = total + parts_in[off]
    times_all[flat] = ratio * total

    def send_row(off):
        peer = lax.rem(flat + off, n * m)
        move(
            times_all.at[flat], times_all.at[flat], row_s, row_r, lax.rem(peer, n), peer // n
        ).start()

    loop(1, n * m, send_row)
    flip(wide, 0)
    wide_copy.wait_recv()
    flip(wide_in, 1)

    all_of(parts_in.at[others], part_s, part_r).wait_send()
    all_of(runs_all.at[others], half_s, half_r).wait_send()
    wide_copy.wait_send()
    all_of(times_all.at[pl.ds(1, n * m - 1)], row_s, row_r).wait_recv()
    for k in range(n * m):
        times_flat[k:k + 1, :] = times_all[k]

    weights = []
    for index in (tm, other):
        low = times_flat[aligned(index, kk), :].astype(BF16).astype(F32)
        weights.extend(low * runs[i:i + 1] for i in range(rows))
    weight = jnp.concatenate(split(jnp.concatenate(weights, axis=0)), axis=1)

    def send_term(index):
        peer = ahead(index)
        move(terms.at[peer], terms_in.at[index], term_s, term_r, peer, tm).start()

    for k in list(range(1, zs)) + [0]:
        to_z = lax.rem(z + k, zs)
        piece = flipped[aligned(to_z, strip), :]
        terms[pl.ds(to_z * QUAD, QUAD)] = fold(dot_low(piece, weight)).reshape(QUAD, block, rank)
        loop(max(k * QUAD, 1), (k + 1) * QUAD, send_term)
    all_of(times_all.at[pl.ds(1, n * m - 1)], row_s, row_r).wait_send()
    time_gram = self_gram(times_flat[...])
    own = bin_ref[aligned(flat, block), :]
    scale = own / dot_f32(own, run_gram * time_gram)

    def narrow(i):
        slabs[1, aligned(i, chunk), :] = wide_in[aligned(i, chunk), :].astype(BF16)

    loop(0, 8, narrow)
    total = terms[me]
    all_of(terms_in.at[others], term_s, term_r).wait_recv()
    for index in range(1, n):
        total = total + terms_in[index]
    bins_all[flat] = scale * total

    def send_bins(index):
        move(
            bins_all.at[flat], bins_all.at[flat], bin_s, bin_r.at[index // QUAD], ahead(index), tm
        ).start()

    loop(1, n, send_bins)
    all_of(terms_in.at[others], term_s, term_r).wait_send()

    def group(core, k):
        return pl.ds(core * n + lax.rem(z - k + zs, zs) * QUAD, QUAD)

    def hand_on(k):
        mine = bins_all.at[group(tm, k)]
        move(mine, mine, pass_s, pass_r, me, other).start()

    all_of(bins_all.at[pl.ds(0, QUAD - 1)], bin_s, bin_r.at[0]).wait_recv()
    hand_on(0)

    def arrive(k):
        all_of(bins_all.at[group(tm, k)], bin_s, bin_r.at[k]).wait_recv()
        hand_on(k)

    loop(1, zs, arrive)

    def use(core, index):
        blocks = pl.ds(core * n, n)
        write = pltpu.make_async_copy(bins_all.at[blocks], bin_out.at[blocks], out_sem.at[index])
        write.start()
        bins = bins_all[blocks].reshape(span, rank)
        bins_low = bins.astype(BF16)
        sums = [dot_low(slabs[off, :, aligned(core, span)], bins_low) for off in range(m)]
        return write, sums, self_gram(bins)

    write_own, own_sums, own_gram = use(tm, 0)
    for off in range(m):
        inner_sum[off] = own_sums[off]
    all_of(bins_all.at[pl.ds(other * n, n)], pass_s, pass_r).wait_recv()
    write_other, other_sums, other_gram = use(other, 1)
    mixing = (own_gram + other_gram) * time_gram
    run_terms = None
    for off, index in enumerate((tm, other)):
        weight = times_flat[aligned(index, kk), :]
        whole = (inner_sum[off] + other_sums[off]).reshape(rows, kk, rank)
        some = jnp.sum(whole * weight[None], axis=1)
        run_terms = some if run_terms is None else run_terms + some
    run_out[...] = runs * run_terms / (dot_f32(runs, mixing) + 1.0 - live)
    time_out[...] = times_flat[aligned(tm, kk), :]
    all_of(bins_all.at[others], bin_s, bin_r.at[0]).wait_send()
    all_of(bins_all.at[pl.ds(0, n)], pass_s, pass_r).wait_send()
    write_own.wait()
    write_other.wait()


def hand_out(run_in, bin_in, time_in, run_out, bin_out, time_out, runs, bins, times, in_s, out_s):
    size = bins.shape[0] // QUAD
    moves = [(run_in, runs, run_out), (time_in, times, time_out)]
    for index in range(QUAD):
        mine = pl.ds(index * size, size)
        moves.append((bin_in.at[mine], bins.at[mine], bin_out.at[mine]))
    loads = [pltpu.make_async_copy(a, b, in_s.at[i]) for i, (a, b, _) in enumerate(moves)]
    stores = [pltpu.make_async_copy(b, c, out_s.at[i]) for i, (_, b, c) in enumerate(moves)]
    for made in loads:
        made.start()
    for load, store in zip(loads, stores):
        load.wait()
        store.start()
    for made in stores:
        made.wait()


def fused(n, m, tensor, run_counts, run_init, bin_init, time_init):
    rows, kk, jj = tensor.shape
    rank = bin_init.shape[1]
    block = jj // (n * m)
    zs = n // QUAD
    dma = pltpu.SemaphoreType.DMA
    vmem = pl.BlockSpec(memory_space=pltpu.VMEM)
    anywhere = pl.BlockSpec(memory_space=pl.ANY)
    shapes = (
        jax.ShapeDtypeStruct((rows, rank), F32),
        jax.ShapeDtypeStruct((n * m, block, rank), F32),
        jax.ShapeDtypeStruct((kk, rank), F32),
    )
    results = pl.pallas_call(
        functools.partial(kernel, n, m),
        out_shape=shapes,
        in_specs=[anywhere] * 5,
        out_specs=(vmem, anywhere, vmem),
        scratch_shapes=[
            pltpu.SMEM((1,), jnp.int32),
            pltpu.VMEM((m, rows * kk, jj), BF16),
            pltpu.VMEM((rows, rank), F32),
            pltpu.VMEM((jj, rank), F32),
            pltpu.VMEM((kk, rank), F32),
            pltpu.VMEM((rows * kk, jj), F32),
            pltpu.VMEM((rows * kk, jj), F32),
            pltpu.VMEM((jj // m, m * rows * kk), BF16),
            pltpu.VMEM((n, block, rank), F32),
            pltpu.VMEM((n, block, rank), F32),
            pltpu.VMEM((n * m, block, rank), F32),
            pltpu.VMEM((m, rows * kk, rank), F32),
            pltpu.VMEM((n, rows, rank), F32),
            pltpu.VMEM((n, 1, rank), F32),
            pltpu.VMEM((n, 1, rank), F32),
            pltpu.VMEM((n * m, 1, rank), F32),
            pltpu.VMEM((n * m, rank), F32),
            dma((5,)), *[dma] * 10, dma, dma((zs,)), dma, dma, dma((m,)),
        ],
        compiler_params=pltpu.CompilerParams(
            collective_id=0, has_side_effects=True, vmem_limit_bytes=VMEM_LIMIT
        ),
    )(run_counts, tensor.reshape(rows * kk, jj), run_init, bin_init, time_init)
    runs, bins, times = pl.pallas_call(
        hand_out,
        out_shape=shapes,
        in_specs=[anywhere] * 3,
        out_specs=[anywhere] * 3,
        scratch_shapes=[pltpu.VMEM(x.shape, F32) for x in shapes] + [dma((2 + QUAD,))] * 2,
        compiler_params=pltpu.CompilerParams(vmem_limit_bytes=VMEM_LIMIT),
    )(*results)
    return runs, bins.reshape(jj, rank), times


def update(n, m, *args):
    rows, kk, jj = args[0].shape
    fits = m == 2 and kk == n and n % QUAD == 0 and kk % 16 == 0 and rows % 8 == 0
    fits = fits and jj % (8 * n * m) == 0 and (QUAD * jj // (n * m)) % 128 == 0
    return fused(n, m, *args) if fits else shards(*args)


def solution(mesh):
    return jax.shard_map(
        functools.partial(update, mesh.shape["runs"], mesh.shape["tm"]),
        mesh=mesh,
        in_specs=(P("runs", "tm", None), P("runs"), P("runs", None), P(), P("tm", None)),
        out_specs=(P("runs", None), P(), P("tm", None)),
        check_vma=False,
    )
```

```python
import functools

import jax
import jax.numpy as jnp
from jax import lax
from jax.experimental import pallas as pl
from jax.experimental.pallas import tpu as pltpu
from jax.sharding import PartitionSpec as P

HIGH = lax.Precision.HIGHEST
STEP_ROWS = 8
MESH = pl.DeviceIdType.MESH
F32 = jnp.float32
BF16 = jnp.bfloat16


def gram(factor):
    return jnp.dot(factor.T, factor, precision=HIGH)


def run_gram_sum(runs):
    return lax.psum(gram(runs), "runs")


def time_gram_sum(times):
    return lax.psum(gram(times), "tm")


def shards(tensor, run_counts, run_init, bin_init, time_init):
    rowcap = tensor.shape[0]
    count = run_counts[0]
    live = (jnp.arange(rowcap, dtype=jnp.int32) < count).astype(F32)[:, None]
    blocks = (count + STEP_ROWS - 1) // STEP_ROWS
    runs = run_init * live
    bins = bin_init
    times = time_init

    def sweep(step, init):
        return lax.fori_loop(0, blocks, lambda index, carry: step(index * STEP_ROWS, carry), init)

    run_gram = run_gram_sum(runs)
    bin_gram = gram(bins)
    bins_low = bins.astype(BF16)

    def step(start, total):
        block = lax.dynamic_slice_in_dim(tensor, start, STEP_ROWS, 0)
        rows = lax.dynamic_slice_in_dim(runs, start, STEP_ROWS, 0)
        inner_sum = jnp.einsum("ikj,jr->ikr", block, bins_low, preferred_element_type=F32)
        return total + jnp.einsum("ir,ikr->kr", rows, inner_sum, precision=HIGH)

    local = sweep(step, jnp.zeros((tensor.shape[1], bins.shape[1]), F32))
    time_terms = lax.psum(local, "runs")
    times = times * time_terms / jnp.dot(times, run_gram * bin_gram, precision=HIGH)
    time_gram = time_gram_sum(times)
    times_low = times.astype(BF16)

    def step(start, total):
        block = lax.dynamic_slice_in_dim(tensor, start, STEP_ROWS, 0)
        rows = lax.dynamic_slice_in_dim(runs, start, STEP_ROWS, 0)
        partial_value = jnp.einsum("ikj,kr->ijr", block, times_low, preferred_element_type=F32)
        return total + jnp.einsum("ir,ijr->jr", rows, partial_value, precision=HIGH)

    local_terms = sweep(step, jnp.zeros((tensor.shape[2], times.shape[1]), F32))
    mixing = run_gram * time_gram
    bin_terms = lax.psum(local_terms, ("runs", "tm"))
    bins = bins * bin_terms / jnp.dot(bins, mixing, precision=HIGH)
    bin_gram = gram(bins)
    run_bins_low = bins.astype(BF16)

    def step(start, total):
        block = lax.dynamic_slice_in_dim(tensor, start, STEP_ROWS, 0)
        inner_sum = jnp.einsum("ikj,jr->ikr", block, run_bins_low, preferred_element_type=F32)
        row_terms = jnp.einsum("kr,ikr->ir", times, inner_sum, precision=HIGH)
        return lax.dynamic_update_slice_in_dim(total, row_terms, start, 0)

    local = sweep(step, jnp.zeros((rowcap, bins.shape[1]), F32))
    run_terms = lax.psum(local, "tm")
    runs = runs * run_terms / (jnp.dot(runs, bin_gram * time_gram, precision=HIGH) + 1.0 - live)
    return (runs, bins, times)


def split(x):
    hi = x.astype(BF16)
    return hi, (x - hi.astype(F32)).astype(BF16)


def dot_low(a, b):
    return lax.dot_general(a, b, (((1,), (0,)), ((), ())), preferred_element_type=F32)


def fold(x):
    half = x.shape[1] // 2
    return x[:, :half] + x[:, half:]


def self_gram(x):
    both = jnp.concatenate(split(x), axis=1)
    product = fold(
        lax.dot_general(both, both, (((0,), (0,)), ((), ())), preferred_element_type=F32)
    )
    half = product.shape[0] // 2
    return product[:half] + product[half:]


def dot_f32(a, b):
    right = jnp.concatenate(split(b), axis=1)
    return fold(
        dot_low(jnp.concatenate(split(a), axis=1), jnp.concatenate([right, right], axis=0))
    )


QUAD = 4
VMEM_LIMIT = 64 * 2**20 - 2**16


def kernel(
    n, m, count_in, tensor_in, run_in, bin_in, time_in,
    run_out, bin_out, time_out,
    count_ref, slabs, run_ref, bin_ref, time_ref,
    wide, wide_in, flipped, terms, terms_in,
    bins_all, inner_sum, gram_sum, runs_all, parts, parts_in, times_all, times_flat,
    load_sem, wide_s, wide_r, half_s, half_r, part_s, part_r, row_s, row_r,
    term_s, term_r, bin_s, bin_r, pass_s, pass_r, out_sem,
):
    me = lax.axis_index("runs")
    tm = lax.axis_index("tm")
    rows = run_ref.shape[0]
    kk = time_ref.shape[0]
    jj, rank = bin_ref.shape
    block = jj // (n * m)
    span = jj // m
    flat = tm * n + me
    zs = n // QUAD
    strip = QUAD * block
    other = 1 - tm
    z = me // QUAD
    q = lax.rem(me, QUAD)

    def ahead(index):
        return lax.rem(z + index // QUAD, zs) * QUAD + lax.rem(q + index, QUAD)

    def move(src, dst, send, recv, run_index, tm_index):
        return pltpu.make_async_remote_copy(
            src_ref=src, dst_ref=dst, send_sem=send, recv_sem=recv,
            device_id=(run_index, tm_index), device_id_type=MESH,
        )

    def all_of(ref, send, recv):
        return move(ref, ref, send, recv, me, other)

    def loop(low, high, body):
        lax.fori_loop(low, high, lambda i, c: (body(i), c)[1], 0)

    def aligned(value, unit):
        return pl.ds(pl.multiple_of(value * unit, unit), unit)

    loads = [
        pltpu.make_async_copy(src, dst, load_sem.at[index])
        for index, (src, dst) in enumerate((
            (tensor_in, slabs.at[0]), (bin_in, bin_ref), (count_in, count_ref),
            (run_in, run_ref), (time_in, time_ref),
        ))
    ]
    for made in loads:
        made.start()

    barrier = pltpu.get_barrier_semaphore()

    def greet(off):
        peer = lax.rem(flat + off, n * m)
        pl.semaphore_signal(
            barrier, inc=1, device_id=(lax.rem(peer, n), peer // n), device_id_type=MESH
        )

    loop(1, n * m, greet)
    for made in loads:
        made.wait()

    live = (lax.broadcasted_iota(jnp.int32, (rows, rank), 0) < count_ref[0]).astype(F32)
    runs = run_ref[...] * live
    runs_all[me] = runs
    inner = dot_low(slabs[0], bin_ref[...].astype(BF16)).reshape(rows, kk, rank)
    upper = inner[0] * runs[0:1]
    for i in range(1, rows):
        upper = upper + inner[i] * runs[i:i + 1]
    for k in range(kk):
        parts[k] = upper[k:k + 1]

    pl.semaphore_wait(barrier, n * m - 1)

    def send_part(off):
        peer = lax.rem(me + off, n)
        move(runs_all.at[me], runs_all.at[me], half_s, half_r, peer, tm).start()
        move(parts.at[peer], parts_in.at[off], part_s, part_r, peer, tm).start()

    loop(1, n, send_part)

    chunk = rows * kk // 8

    def widen(core):
        def step(i):
            wide[core, aligned(i, chunk), :] = slabs[
                0, aligned(i, chunk), aligned(core, span)
            ].astype(F32)

        loop(0, 8, step)

    widen(other)
    wide_copy = move(wide.at[other], wide_in.at[other], wide_s.at[0], wide_r.at[0], me, other)
    wide_copy.start()
    widen(tm)
    rest_copy = move(wide.at[tm], wide_in.at[tm], wide_s.at[1], wide_r.at[1], me, other)

    bin_gram = self_gram(bin_ref[...])

    def flip(source, place):
        def step(i):
            flipped[aligned(i, strip), place * rows * kk:(place + 1) * rows * kk] = (
                source[tm, :, aligned(i, strip)].T.astype(BF16)
            )

        loop(0, span // strip, step)

    flip(wide, 0)
    others = pl.ds(1, n - 1)
    all_of(runs_all.at[others], half_s, half_r).wait_recv()
    run_gram = self_gram(runs_all[...].reshape(n * rows, rank))
    lower = dot_f32(time_ref[...], run_gram * bin_gram)
    times_flat[pl.ds(0, kk), :] = time_ref[...] / lower
    ratio = times_flat[pl.ds(me, 1), :]
    all_of(parts_in.at[others], part_s, part_r).wait_recv()
    total = parts[me]
    for off in range(1, n):
        total = total + parts_in[off]
    times_all[flat] = ratio * total

    def send_row(off):
        peer = lax.rem(flat + off, n * m)
        move(
            times_all.at[flat], times_all.at[flat], row_s, row_r, lax.rem(peer, n), peer // n
        ).start()

    loop(1, n * m, send_row)
    wide_copy.wait_recv()
    flip(wide_in, 1)

    all_of(parts_in.at[others], part_s, part_r).wait_send()
    all_of(runs_all.at[others], half_s, half_r).wait_send()
    wide_copy.wait_send()
    all_of(times_all.at[pl.ds(1, n * m - 1)], row_s, row_r).wait_recv()
    for k in range(n * m):
        times_flat[k:k + 1, :] = times_all[k]

    weights = []
    for index in (tm, other):
        low = times_flat[aligned(index, kk), :].astype(BF16).astype(F32)
        weights.extend(low * runs[i:i + 1] for i in range(rows))
    weight = jnp.concatenate(split(jnp.concatenate(weights, axis=0)), axis=1)

    def send_term(index):
        peer = ahead(index)
        move(terms.at[peer], terms_in.at[index], term_s, term_r, peer, tm).start()

    for k in list(range(1, zs)) + [0]:
        to_z = lax.rem(z + k, zs)
        piece = flipped[aligned(to_z, strip), :]
        terms[pl.ds(to_z * QUAD, QUAD)] = fold(dot_low(piece, weight)).reshape(QUAD, block, rank)
        loop(max(k * QUAD, 1), (k + 1) * QUAD, send_term)
    rest_copy.start()
    all_of(times_all.at[pl.ds(1, n * m - 1)], row_s, row_r).wait_send()
    time_gram = self_gram(times_flat[...])
    own = bin_ref[aligned(flat, block), :]
    scale = own / dot_f32(own, run_gram * time_gram)

    def narrow(core):
        def step(i):
            slabs[1, aligned(i, chunk), aligned(core, span)] = wide_in[
                core, aligned(i, chunk), :
            ].astype(BF16)

        loop(0, 8, step)

    narrow(tm)
    gram_sum[...] = jnp.zeros_like(gram_sum)
    inner_sum[...] = jnp.zeros_like(inner_sum)
    total = terms[me]
    all_of(terms_in.at[others], term_s, term_r).wait_recv()
    for index in range(1, n):
        total = total + terms_in[index]
    bins_all[flat] = scale * total

    def send_bins(index):
        move(
            bins_all.at[flat], bins_all.at[flat], bin_s, bin_r.at[index // QUAD], ahead(index), tm
        ).start()

    loop(1, n, send_bins)
    rest_copy.wait()
    narrow(other)
    all_of(terms_in.at[others], term_s, term_r).wait_send()

    def group(core, k):
        return pl.ds(core * n + lax.rem(z - k + zs, zs) * QUAD, QUAD)

    def hand_on(k):
        mine = bins_all.at[group(tm, k)]
        move(mine, mine, pass_s, pass_r.at[k], me, other).start()

    all_of(bins_all.at[pl.ds(0, QUAD - 1)], bin_s, bin_r.at[0]).wait_recv()
    hand_on(0)

    def arrive(k):
        all_of(bins_all.at[group(tm, k)], bin_s, bin_r.at[k]).wait_recv()
        hand_on(k)

    loop(1, zs, arrive)

    def use(k):
        from_z = lax.rem(z - k + zs, zs)
        all_of(bins_all.at[group(other, k)], pass_s, pass_r.at[k]).wait_recv()
        pieces = []
        for core in range(m):
            mine = group(core, k)
            pieces.append(bins_all[mine].reshape(strip, rank))
            pltpu.make_async_copy(bins_all.at[mine], bin_out.at[mine], out_sem.at[k, core]).start()
        bins = jnp.concatenate(pieces, axis=0)
        bins_low = bins.astype(BF16)
        gram_sum[...] += self_gram(bins)
        for off in range(m):
            slab = jnp.concatenate(
                [slabs[off, :, aligned(core * zs + from_z, strip)] for core in range(m)], axis=1
            )
            inner_sum[off] += dot_low(slab, bins_low)

    loop(0, zs, use)
    run_terms = None
    for off, index in enumerate((tm, other)):
        weight = times_flat[aligned(index, kk), :]
        some = jnp.sum(inner_sum[off].reshape(rows, kk, rank) * weight[None], axis=1)
        run_terms = some if run_terms is None else run_terms + some
    run_out[...] = runs * run_terms / (dot_f32(runs, gram_sum[...] * time_gram) + 1.0 - live)
    time_out[...] = times_flat[aligned(tm, kk), :]
    all_of(bins_all.at[others], bin_s, bin_r.at[0]).wait_send()
    all_of(bins_all.at[pl.ds(0, n)], pass_s, pass_r.at[0]).wait_send()

    def finish(k):
        for core in range(m):
            mine = group(core, k)
            pltpu.make_async_copy(bins_all.at[mine], bin_out.at[mine], out_sem.at[k, core]).wait()

    loop(0, zs, finish)


def hand_out(run_in, bin_in, time_in, run_out, bin_out, time_out, runs, bins, times, in_s, out_s):
    size = bins.shape[0] // QUAD
    moves = [(run_in, runs, run_out), (time_in, times, time_out)]
    for index in range(QUAD):
        mine = pl.ds(index * size, size)
        moves.append((bin_in.at[mine], bins.at[mine], bin_out.at[mine]))
    loads = [pltpu.make_async_copy(a, b, in_s.at[i]) for i, (a, b, _) in enumerate(moves)]
    stores = [pltpu.make_async_copy(b, c, out_s.at[i]) for i, (_, b, c) in enumerate(moves)]
    for made in loads:
        made.start()
    for load, store in zip(loads, stores):
        load.wait()
        store.start()
    for made in stores:
        made.wait()


def fused(n, m, tensor, run_counts, run_init, bin_init, time_init):
    rows, kk, jj = tensor.shape
    rank = bin_init.shape[1]
    block = jj // (n * m)
    zs = n // QUAD
    dma = pltpu.SemaphoreType.DMA
    vmem = pl.BlockSpec(memory_space=pltpu.VMEM)
    anywhere = pl.BlockSpec(memory_space=pl.ANY)
    shapes = (
        jax.ShapeDtypeStruct((rows, rank), F32),
        jax.ShapeDtypeStruct((n * m, block, rank), F32),
        jax.ShapeDtypeStruct((kk, rank), F32),
    )
    results = pl.pallas_call(
        functools.partial(kernel, n, m),
        out_shape=shapes,
        in_specs=[anywhere] * 5,
        out_specs=(vmem, anywhere, vmem),
        scratch_shapes=[
            pltpu.SMEM((1,), jnp.int32),
            pltpu.VMEM((m, rows * kk, jj), BF16),
            pltpu.VMEM((rows, rank), F32),
            pltpu.VMEM((jj, rank), F32),
            pltpu.VMEM((kk, rank), F32),
            pltpu.VMEM((m, rows * kk, jj // m), F32),
            pltpu.VMEM((m, rows * kk, jj // m), F32),
            pltpu.VMEM((jj // m, m * rows * kk), BF16),
            pltpu.VMEM((n, block, rank), F32),
            pltpu.VMEM((n, block, rank), F32),
            pltpu.VMEM((n * m, block, rank), F32),
            pltpu.VMEM((m, rows * kk, rank), F32),
            pltpu.VMEM((rank, rank), F32),
            pltpu.VMEM((n, rows, rank), F32),
            pltpu.VMEM((n, 1, rank), F32),
            pltpu.VMEM((n, 1, rank), F32),
            pltpu.VMEM((n * m, 1, rank), F32),
            pltpu.VMEM((n * m, rank), F32),
            dma((5,)), dma((2,)), dma((2,)), *[dma] * 8, dma, dma((zs,)), dma, dma((zs,)), dma((zs, m)),
        ],
        compiler_params=pltpu.CompilerParams(
            collective_id=0, has_side_effects=True, vmem_limit_bytes=VMEM_LIMIT
        ),
    )(run_counts, tensor.reshape(rows * kk, jj), run_init, bin_init, time_init)
    runs, bins, times = pl.pallas_call(
        hand_out,
        out_shape=shapes,
        in_specs=[anywhere] * 3,
        out_specs=[anywhere] * 3,
        scratch_shapes=[pltpu.VMEM(x.shape, F32) for x in shapes] + [dma((2 + QUAD,))] * 2,
        compiler_params=pltpu.CompilerParams(vmem_limit_bytes=VMEM_LIMIT),
    )(*results)
    return runs, bins.reshape(jj, rank), times


def update(n, m, *args):
    rows, kk, jj = args[0].shape
    fits = m == 2 and kk == n and n % QUAD == 0 and kk % 16 == 0 and rows % 8 == 0
    fits = fits and jj % (8 * n * m) == 0 and (QUAD * jj // (n * m)) % 128 == 0
    return fused(n, m, *args) if fits else shards(*args)


def solution(mesh):
    return jax.shard_map(
        functools.partial(update, mesh.shape["runs"], mesh.shape["tm"]),
        mesh=mesh,
        in_specs=(P("runs", "tm", None), P("runs"), P("runs", None), P(), P("tm", None)),
        out_specs=(P("runs", None), P(), P("tm", None)),
        check_vma=False,
    )
```

```python
import functools

import jax
import jax.numpy as jnp
from jax import lax
from jax.experimental import pallas as pl
from jax.experimental.pallas import tpu as pltpu
from jax.sharding import PartitionSpec as P

HIGH = lax.Precision.HIGHEST
STEP_ROWS = 8
MESH = pl.DeviceIdType.MESH
F32 = jnp.float32
BF16 = jnp.bfloat16


def gram(factor):
    return jnp.dot(factor.T, factor, precision=HIGH)


def run_gram_sum(runs):
    return lax.psum(gram(runs), "runs")


def time_gram_sum(times):
    return lax.psum(gram(times), "tm")


def shards(tensor, run_counts, run_init, bin_init, time_init):
    rowcap = tensor.shape[0]
    count = run_counts[0]
    live = (jnp.arange(rowcap, dtype=jnp.int32) < count).astype(F32)[:, None]
    blocks = (count + STEP_ROWS - 1) // STEP_ROWS
    runs = run_init * live
    bins = bin_init
    times = time_init

    def sweep(step, init):
        return lax.fori_loop(0, blocks, lambda index, carry: step(index * STEP_ROWS, carry), init)

    run_gram = run_gram_sum(runs)
    bin_gram = gram(bins)
    bins_low = bins.astype(BF16)

    def step(start, total):
        block = lax.dynamic_slice_in_dim(tensor, start, STEP_ROWS, 0)
        rows = lax.dynamic_slice_in_dim(runs, start, STEP_ROWS, 0)
        inner_sum = jnp.einsum("ikj,jr->ikr", block, bins_low, preferred_element_type=F32)
        return total + jnp.einsum("ir,ikr->kr", rows, inner_sum, precision=HIGH)

    local = sweep(step, jnp.zeros((tensor.shape[1], bins.shape[1]), F32))
    time_terms = lax.psum(local, "runs")
    times = times * time_terms / jnp.dot(times, run_gram * bin_gram, precision=HIGH)
    time_gram = time_gram_sum(times)
    times_low = times.astype(BF16)

    def step(start, total):
        block = lax.dynamic_slice_in_dim(tensor, start, STEP_ROWS, 0)
        rows = lax.dynamic_slice_in_dim(runs, start, STEP_ROWS, 0)
        partial_value = jnp.einsum("ikj,kr->ijr", block, times_low, preferred_element_type=F32)
        return total + jnp.einsum("ir,ijr->jr", rows, partial_value, precision=HIGH)

    local_terms = sweep(step, jnp.zeros((tensor.shape[2], times.shape[1]), F32))
    mixing = run_gram * time_gram
    bin_terms = lax.psum(local_terms, ("runs", "tm"))
    bins = bins * bin_terms / jnp.dot(bins, mixing, precision=HIGH)
    bin_gram = gram(bins)
    run_bins_low = bins.astype(BF16)

    def step(start, total):
        block = lax.dynamic_slice_in_dim(tensor, start, STEP_ROWS, 0)
        inner_sum = jnp.einsum("ikj,jr->ikr", block, run_bins_low, preferred_element_type=F32)
        row_terms = jnp.einsum("kr,ikr->ir", times, inner_sum, precision=HIGH)
        return lax.dynamic_update_slice_in_dim(total, row_terms, start, 0)

    local = sweep(step, jnp.zeros((rowcap, bins.shape[1]), F32))
    run_terms = lax.psum(local, "tm")
    runs = runs * run_terms / (jnp.dot(runs, bin_gram * time_gram, precision=HIGH) + 1.0 - live)
    return (runs, bins, times)


def split(x):
    hi = x.astype(BF16)
    return hi, (x - hi.astype(F32)).astype(BF16)


def dot_low(a, b):
    return lax.dot_general(a, b, (((1,), (0,)), ((), ())), preferred_element_type=F32)


def fold(x):
    half = x.shape[1] // 2
    return x[:, :half] + x[:, half:]


def self_gram(x):
    both = jnp.concatenate(split(x), axis=1)
    product = fold(
        lax.dot_general(both, both, (((0,), (0,)), ((), ())), preferred_element_type=F32)
    )
    half = product.shape[0] // 2
    return product[:half] + product[half:]


def dot_f32(a, b):
    right = jnp.concatenate(split(b), axis=1)
    return fold(
        dot_low(jnp.concatenate(split(a), axis=1), jnp.concatenate([right, right], axis=0))
    )


QUAD = 4
VMEM_LIMIT = 64 * 2**20 - 2**16


def kernel(
    n, m, count_in, tensor_in, run_in, bin_in, time_in,
    run_out, bin_out, time_out,
    count_ref, slabs, run_ref, bin_ref, time_ref,
    wide, wide_in, flipped, terms, terms_in,
    bins_all, inner_sum, gram_sum, halves, parts, parts_in, times_all, times_flat,
    load_sem, wide_s, wide_r, half_s, half_r, fwd_s, fwd_r, part_s, part_r, row_s, row_r,
    term_s, term_r, bin_s, bin_r, pass_s, pass_r, out_sem,
):
    me = lax.axis_index("runs")
    tm = lax.axis_index("tm")
    rows = run_ref.shape[0]
    kk = time_ref.shape[0]
    jj, rank = bin_ref.shape
    block = jj // (n * m)
    half = rows // m
    span = jj // m
    flat = tm * n + me
    zs = n // QUAD
    strip = QUAD * block
    other = 1 - tm
    z = me // QUAD
    q = lax.rem(me, QUAD)

    def ahead(index):
        return lax.rem(z + index // QUAD, zs) * QUAD + lax.rem(q + index, QUAD)

    def move(src, dst, send, recv, run_index, tm_index):
        return pltpu.make_async_remote_copy(
            src_ref=src, dst_ref=dst, send_sem=send, recv_sem=recv,
            device_id=(run_index, tm_index), device_id_type=MESH,
        )

    def all_of(ref, send, recv):
        return move(ref, ref, send, recv, me, other)

    def loop(low, high, body):
        lax.fori_loop(low, high, lambda i, c: (body(i), c)[1], 0)

    def aligned(value, unit):
        return pl.ds(pl.multiple_of(value * unit, unit), unit)

    loads = [
        pltpu.make_async_copy(src, dst, load_sem.at[index])
        for index, (src, dst) in enumerate((
            (tensor_in, slabs.at[0]), (bin_in, bin_ref), (count_in, count_ref),
            (run_in, run_ref), (time_in, time_ref),
        ))
    ]
    for made in loads:
        made.start()

    barrier = pltpu.get_barrier_semaphore()

    def greet(off):
        peer = lax.rem(flat + off, n * m)
        pl.semaphore_signal(
            barrier, inc=1, device_id=(lax.rem(peer, n), peer // n), device_id_type=MESH
        )

    loop(1, n * m, greet)
    for made in loads:
        made.wait()

    live = (lax.broadcasted_iota(jnp.int32, (rows, rank), 0) < count_ref[0]).astype(F32)
    runs = run_ref[...] * live
    halves[flat] = jnp.where(tm == 0, runs[:half], runs[rows - half:])
    inner = dot_low(slabs[0], bin_ref[...].astype(BF16)).reshape(rows, kk, rank)
    upper = inner[0] * runs[0:1]
    for i in range(1, rows):
        upper = upper + inner[i] * runs[i:i + 1]
    lower = dot_f32(time_ref[...], self_gram(runs) * self_gram(bin_ref[...]))
    both = jnp.concatenate([upper, lower], axis=1)
    for k in range(kk):
        parts[k] = both[k:k + 1]

    pl.semaphore_wait(barrier, n * m - 1)

    def send_part(off):
        peer = lax.rem(me + off, n)
        move(parts.at[peer], parts_in.at[off], part_s, part_r, peer, tm).start()

    loop(1, n, send_part)

    chunk = rows * kk // 8

    def widen(i):
        wide[aligned(i, chunk), :] = slabs[0, aligned(i, chunk), :].astype(F32)

    loop(0, 8, widen)
    wide_copy = move(wide, wide_in, wide_s, wide_r, me, other)
    wide_copy.start()

    def send_half(off):
        peer = lax.rem(me + off, n)
        move(halves.at[flat], halves.at[flat], half_s, half_r, peer, tm).start()

    loop(1, n, send_half)

    def flip(source, place):
        def step(i):
            columns = aligned(tm * (span // strip) + i, strip)
            flipped[aligned(i, strip), place * rows * kk:(place + 1) * rows * kk] = (
                source[:, columns].T.astype(BF16)
            )

        loop(0, span // strip, step)

    flip(wide, 0)

    others = pl.ds(1, n - 1)
    all_of(parts_in.at[others], part_s, part_r).wait_recv()
    total = parts[me]
    for off in range(1, n):
        total = total + parts_in[off]
    times_all[flat] = time_ref[pl.ds(me, 1), :] * total[:, :rank] / total[:, rank:]

    def send_row(off):
        peer = lax.rem(flat + off, n * m)
        move(
            times_all.at[flat], times_all.at[flat], row_s, row_r, lax.rem(peer, n), peer // n
        ).start()

    loop(1, n * m, send_row)
    all_of(halves.at[others], half_s, half_r).wait_recv()
    mine = pl.ds(tm * n, n)
    fwd_copy = move(halves.at[mine], halves.at[mine], fwd_s, fwd_r, me, other)
    fwd_copy.start()
    wide_copy.wait_recv()
    flip(wide_in, 1)

    all_of(parts_in.at[others], part_s, part_r).wait_send()
    all_of(halves.at[others], half_s, half_r).wait_send()
    wide_copy.wait_send()
    all_of(times_all.at[pl.ds(1, n * m - 1)], row_s, row_r).wait_recv()
    for k in range(n * m):
        times_flat[k:k + 1, :] = times_all[k]

    weights = []
    for index in (tm, other):
        low = times_flat[aligned(index, kk), :].astype(BF16).astype(F32)
        weights.extend(low * runs[i:i + 1] for i in range(rows))
    weight = jnp.concatenate(split(jnp.concatenate(weights, axis=0)), axis=1)

    def send_term(index):
        peer = ahead(index)
        move(terms.at[peer], terms_in.at[index], term_s, term_r, peer, tm).start()

    for k in list(range(1, zs)) + [0]:
        to_z = lax.rem(z + k, zs)
        piece = flipped[aligned(to_z, strip), :]
        terms[pl.ds(to_z * QUAD, QUAD)] = fold(dot_low(piece, weight)).reshape(QUAD, block, rank)
        loop(max(k * QUAD, 1), (k + 1) * QUAD, send_term)
    all_of(times_all.at[pl.ds(1, n * m - 1)], row_s, row_r).wait_send()
    fwd_copy.wait()
    run_gram = self_gram(halves[...].reshape(n * m * half, rank))
    time_gram = self_gram(times_flat[...])
    own = bin_ref[aligned(flat, block), :]
    scale = own / dot_f32(own, run_gram * time_gram)

    def narrow(i):
        slabs[1, aligned(i, chunk), :] = wide_in[aligned(i, chunk), :].astype(BF16)

    loop(0, 8, narrow)
    gram_sum[...] = jnp.zeros_like(gram_sum)
    inner_sum[...] = jnp.zeros_like(inner_sum)
    total = terms[me]
    all_of(terms_in.at[others], term_s, term_r).wait_recv()
    for index in range(1, n):
        total = total + terms_in[index]
    bins_all[flat] = scale * total

    def send_bins(index):
        move(
            bins_all.at[flat], bins_all.at[flat], bin_s, bin_r.at[index // QUAD], ahead(index), tm
        ).start()

    loop(1, n, send_bins)
    all_of(terms_in.at[others], term_s, term_r).wait_send()

    def group(core, k):
        return pl.ds(core * n + lax.rem(z - k + zs, zs) * QUAD, QUAD)

    def hand_on(k):
        mine = bins_all.at[group(tm, k)]
        move(mine, mine, pass_s, pass_r.at[k], me, other).start()

    all_of(bins_all.at[pl.ds(0, QUAD - 1)], bin_s, bin_r.at[0]).wait_recv()
    hand_on(0)

    def arrive(k):
        all_of(bins_all.at[group(tm, k)], bin_s, bin_r.at[k]).wait_recv()
        hand_on(k)

    loop(1, zs, arrive)

    def use(k):
        from_z = lax.rem(z - k + zs, zs)
        all_of(bins_all.at[group(other, k)], pass_s, pass_r.at[k]).wait_recv()
        pieces = []
        for core in range(m):
            mine = group(core, k)
            pieces.append(bins_all[mine].reshape(strip, rank))
            pltpu.make_async_copy(bins_all.at[mine], bin_out.at[mine], out_sem.at[k, core]).start()
        bins = jnp.concatenate(pieces, axis=0)
        bins_low = bins.astype(BF16)
        gram_sum[...] += self_gram(bins)
        for off in range(m):
            slab = jnp.concatenate(
                [slabs[off, :, aligned(core * zs + from_z, strip)] for core in range(m)], axis=1
            )
            inner_sum[off] += dot_low(slab, bins_low)

    loop(0, zs, use)
    run_terms = None
    for off, index in enumerate((tm, other)):
        weight = times_flat[aligned(index, kk), :]
        some = jnp.sum(inner_sum[off].reshape(rows, kk, rank) * weight[None], axis=1)
        run_terms = some if run_terms is None else run_terms + some
    run_out[...] = runs * run_terms / (dot_f32(runs, gram_sum[...] * time_gram) + 1.0 - live)
    time_out[...] = times_flat[aligned(tm, kk), :]
    all_of(bins_all.at[others], bin_s, bin_r.at[0]).wait_send()
    all_of(bins_all.at[mine], pass_s, pass_r.at[0]).wait_send()

    def finish(k):
        for core in range(m):
            mine = group(core, k)
            pltpu.make_async_copy(bins_all.at[mine], bin_out.at[mine], out_sem.at[k, core]).wait()

    loop(0, zs, finish)


def hand_out(run_in, bin_in, time_in, run_out, bin_out, time_out, runs, bins, times, in_s, out_s):
    size = bins.shape[0] // QUAD
    moves = [(run_in, runs, run_out), (time_in, times, time_out)]
    for index in range(QUAD):
        mine = pl.ds(index * size, size)
        moves.append((bin_in.at[mine], bins.at[mine], bin_out.at[mine]))
    loads = [pltpu.make_async_copy(a, b, in_s.at[i]) for i, (a, b, _) in enumerate(moves)]
    stores = [pltpu.make_async_copy(b, c, out_s.at[i]) for i, (_, b, c) in enumerate(moves)]
    for made in loads:
        made.start()
    for load, store in zip(loads, stores):
        load.wait()
        store.start()
    for made in stores:
        made.wait()


def fused(n, m, tensor, run_counts, run_init, bin_init, time_init):
    rows, kk, jj = tensor.shape
    rank = bin_init.shape[1]
    block = jj // (n * m)
    half = rows // m
    zs = n // QUAD
    dma = pltpu.SemaphoreType.DMA
    vmem = pl.BlockSpec(memory_space=pltpu.VMEM)
    anywhere = pl.BlockSpec(memory_space=pl.ANY)
    shapes = (
        jax.ShapeDtypeStruct((rows, rank), F32),
        jax.ShapeDtypeStruct((n * m, block, rank), F32),
        jax.ShapeDtypeStruct((kk, rank), F32),
    )
    results = pl.pallas_call(
        functools.partial(kernel, n, m),
        out_shape=shapes,
        in_specs=[anywhere] * 5,
        out_specs=(vmem, anywhere, vmem),
        scratch_shapes=[
            pltpu.SMEM((1,), jnp.int32),
            pltpu.VMEM((m, rows * kk, jj), BF16),
            pltpu.VMEM((rows, rank), F32),
            pltpu.VMEM((jj, rank), F32),
            pltpu.VMEM((kk, rank), F32),
            pltpu.VMEM((rows * kk, jj), F32),
            pltpu.VMEM((rows * kk, jj), F32),
            pltpu.VMEM((jj // m, m * rows * kk), BF16),
            pltpu.VMEM((n, block, rank), F32),
            pltpu.VMEM((n, block, rank), F32),
            pltpu.VMEM((n * m, block, rank), F32),
            pltpu.VMEM((m, rows * kk, rank), F32),
            pltpu.VMEM((rank, rank), F32),
            pltpu.VMEM((n * m, half, rank), F32),
            pltpu.VMEM((n, 1, 2 * rank), F32),
            pltpu.VMEM((n, 1, 2 * rank), F32),
            pltpu.VMEM((n * m, 1, rank), F32),
            pltpu.VMEM((n * m, rank), F32),
            dma((5,)), *[dma] * 12, dma, dma((zs,)), dma, dma((zs,)), dma((zs, m)),
        ],
        compiler_params=pltpu.CompilerParams(
            collective_id=0, has_side_effects=True, vmem_limit_bytes=VMEM_LIMIT
        ),
    )(run_counts, tensor.reshape(rows * kk, jj), run_init, bin_init, time_init)
    runs, bins, times = pl.pallas_call(
        hand_out,
        out_shape=shapes,
        in_specs=[anywhere] * 3,
        out_specs=[anywhere] * 3,
        scratch_shapes=[pltpu.VMEM(x.shape, F32) for x in shapes] + [dma((2 + QUAD,))] * 2,
        compiler_params=pltpu.CompilerParams(vmem_limit_bytes=VMEM_LIMIT),
    )(*results)
    return runs, bins.reshape(jj, rank), times


def update(n, m, *args):
    rows, kk, jj = args[0].shape
    fits = m == 2 and kk == n and n % QUAD == 0 and kk % 16 == 0 and rows % (8 * m) == 0
    fits = fits and jj % (8 * n * m) == 0 and (QUAD * jj // (n * m)) % 128 == 0
    return fused(n, m, *args) if fits else shards(*args)


def solution(mesh):
    return jax.shard_map(
        functools.partial(update, mesh.shape["runs"], mesh.shape["tm"]),
        mesh=mesh,
        in_specs=(P("runs", "tm", None), P("runs"), P("runs", None), P(), P("tm", None)),
        out_specs=(P("runs", None), P(), P("tm", None)),
        check_vma=False,
    )
```

```python
import functools

import jax
import jax.numpy as jnp
from jax import lax
from jax.experimental import pallas as pl
from jax.experimental.pallas import tpu as pltpu
from jax.sharding import PartitionSpec as P

HIGH = lax.Precision.HIGHEST
STEP_ROWS = 8
MESH = pl.DeviceIdType.MESH
F32 = jnp.float32
BF16 = jnp.bfloat16


def gram(factor):
    return jnp.dot(factor.T, factor, precision=HIGH)


def run_gram_sum(runs):
    return lax.psum(gram(runs), "runs")


def time_gram_sum(times):
    return lax.psum(gram(times), "tm")


def shards(tensor, run_counts, run_init, bin_init, time_init):
    rowcap = tensor.shape[0]
    count = run_counts[0]
    live = (jnp.arange(rowcap, dtype=jnp.int32) < count).astype(F32)[:, None]
    blocks = (count + STEP_ROWS - 1) // STEP_ROWS
    runs = run_init * live
    bins = bin_init
    times = time_init

    def sweep(step, init):
        return lax.fori_loop(0, blocks, lambda index, carry: step(index * STEP_ROWS, carry), init)

    run_gram = run_gram_sum(runs)
    bin_gram = gram(bins)
    bins_low = bins.astype(BF16)

    def step(start, total):
        block = lax.dynamic_slice_in_dim(tensor, start, STEP_ROWS, 0)
        rows = lax.dynamic_slice_in_dim(runs, start, STEP_ROWS, 0)
        inner_sum = jnp.einsum("ikj,jr->ikr", block, bins_low, preferred_element_type=F32)
        return total + jnp.einsum("ir,ikr->kr", rows, inner_sum, precision=HIGH)

    local = sweep(step, jnp.zeros((tensor.shape[1], bins.shape[1]), F32))
    time_terms = lax.psum(local, "runs")
    times = times * time_terms / jnp.dot(times, run_gram * bin_gram, precision=HIGH)
    time_gram = time_gram_sum(times)
    times_low = times.astype(BF16)

    def step(start, total):
        block = lax.dynamic_slice_in_dim(tensor, start, STEP_ROWS, 0)
        rows = lax.dynamic_slice_in_dim(runs, start, STEP_ROWS, 0)
        partial_value = jnp.einsum("ikj,kr->ijr", block, times_low, preferred_element_type=F32)
        return total + jnp.einsum("ir,ijr->jr", rows, partial_value, precision=HIGH)

    local_terms = sweep(step, jnp.zeros((tensor.shape[2], times.shape[1]), F32))
    mixing = run_gram * time_gram
    bin_terms = lax.psum(local_terms, ("runs", "tm"))
    bins = bins * bin_terms / jnp.dot(bins, mixing, precision=HIGH)
    bin_gram = gram(bins)
    run_bins_low = bins.astype(BF16)

    def step(start, total):
        block = lax.dynamic_slice_in_dim(tensor, start, STEP_ROWS, 0)
        inner_sum = jnp.einsum("ikj,jr->ikr", block, run_bins_low, preferred_element_type=F32)
        row_terms = jnp.einsum("kr,ikr->ir", times, inner_sum, precision=HIGH)
        return lax.dynamic_update_slice_in_dim(total, row_terms, start, 0)

    local = sweep(step, jnp.zeros((rowcap, bins.shape[1]), F32))
    run_terms = lax.psum(local, "tm")
    runs = runs * run_terms / (jnp.dot(runs, bin_gram * time_gram, precision=HIGH) + 1.0 - live)
    return (runs, bins, times)


def split(x):
    hi = x.astype(BF16)
    return hi, (x - hi.astype(F32)).astype(BF16)


def dot_low(a, b):
    return lax.dot_general(a, b, (((1,), (0,)), ((), ())), preferred_element_type=F32)


def fold(x):
    half = x.shape[1] // 2
    return x[:, :half] + x[:, half:]


def self_gram(x):
    both = jnp.concatenate(split(x), axis=1)
    product = fold(
        lax.dot_general(both, both, (((0,), (0,)), ((), ())), preferred_element_type=F32)
    )
    half = product.shape[0] // 2
    return product[:half] + product[half:]


def dot_f32(a, b):
    right = jnp.concatenate(split(b), axis=1)
    return fold(
        dot_low(jnp.concatenate(split(a), axis=1), jnp.concatenate([right, right], axis=0))
    )


QUAD = 4
VMEM_LIMIT = 64 * 2**20 - 2**16


def kernel(
    n, m, count_in, tensor_in, run_in, bin_in, time_in,
    run_out, bin_out, time_out,
    count_ref, slabs, run_ref, bin_ref, time_ref,
    wide, wide_in, flipped, terms, terms_in,
    bins_all, inner_sum, gram_sum, halves, parts, parts_in, times_all, times_flat,
    load_sem, wide_s, wide_r, half_s, half_r, fwd_s, fwd_r, part_s, part_r, row_s, row_r,
    term_s, term_r, bin_s, bin_r, pass_s, pass_r, out_sem,
):
    me = lax.axis_index("runs")
    tm = lax.axis_index("tm")
    rows = run_ref.shape[0]
    kk = time_ref.shape[0]
    jj, rank = bin_ref.shape
    block = jj // (n * m)
    half = rows // m
    span = jj // m
    flat = tm * n + me
    zs = n // QUAD
    strip = QUAD * block
    other = 1 - tm
    z = me // QUAD
    q = lax.rem(me, QUAD)

    def ahead(index):
        return lax.rem(z + index // QUAD, zs) * QUAD + lax.rem(q + index, QUAD)

    def move(src, dst, send, recv, run_index, tm_index):
        return pltpu.make_async_remote_copy(
            src_ref=src, dst_ref=dst, send_sem=send, recv_sem=recv,
            device_id=(run_index, tm_index), device_id_type=MESH,
        )

    def all_of(ref, send, recv):
        return move(ref, ref, send, recv, me, other)

    def loop(low, high, body, unroll=1):
        lax.fori_loop(low, high, lambda i, c: (body(i), c)[1], 0, unroll=unroll)

    def aligned(value, unit):
        return pl.ds(pl.multiple_of(value * unit, unit), unit)

    loads = [
        pltpu.make_async_copy(src, dst, load_sem.at[index])
        for index, (src, dst) in enumerate((
            (tensor_in, slabs.at[0]), (bin_in, bin_ref), (count_in, count_ref),
            (run_in, run_ref), (time_in, time_ref),
        ))
    ]
    for made in loads:
        made.start()

    barrier = pltpu.get_barrier_semaphore()

    def greet(off):
        peer = lax.rem(flat + off, n * m)
        pl.semaphore_signal(
            barrier, inc=1, device_id=(lax.rem(peer, n), peer // n), device_id_type=MESH
        )

    loop(1, n * m, greet)
    for made in loads:
        made.wait()

    live = (lax.broadcasted_iota(jnp.int32, (rows, rank), 0) < count_ref[0]).astype(F32)
    runs = run_ref[...] * live
    halves[flat] = jnp.where(tm == 0, runs[:half], runs[rows - half:])
    inner = dot_low(slabs[0], bin_ref[...].astype(BF16)).reshape(rows, kk, rank)
    upper = inner[0] * runs[0:1]
    for i in range(1, rows):
        upper = upper + inner[i] * runs[i:i + 1]
    lower = dot_f32(time_ref[...], self_gram(runs) * self_gram(bin_ref[...]))
    both = jnp.concatenate([upper, lower], axis=1)
    for k in range(kk):
        parts[k] = both[k:k + 1]

    pl.semaphore_wait(barrier, n * m - 1)

    def send_part(off):
        peer = lax.rem(me + off, n)
        move(parts.at[peer], parts_in.at[off], part_s, part_r, peer, tm).start()

    loop(1, n, send_part, 5 if n % 5 == 1 else 1)

    chunk = rows * kk // 8

    def widen(i):
        wide[aligned(i, chunk), :] = slabs[0, aligned(i, chunk), :].astype(F32)

    loop(0, 8, widen)
    wide_copy = move(wide, wide_in, wide_s, wide_r, me, other)
    wide_copy.start()

    def send_half(off):
        peer = lax.rem(me + off, n)
        move(halves.at[flat], halves.at[flat], half_s, half_r, peer, tm).start()

    loop(1, n, send_half)

    def flip(source, place):
        def step(i):
            columns = aligned(tm * (span // strip) + i, strip)
            flipped[aligned(i, strip), place * rows * kk:(place + 1) * rows * kk] = (
                source[:, columns].T.astype(BF16)
            )

        loop(0, span // strip, step)

    flip(wide, 0)

    others = pl.ds(1, n - 1)
    all_of(parts_in.at[others], part_s, part_r).wait_recv()
    total = parts[me]
    for off in range(1, n):
        total = total + parts_in[off]
    times_all[flat] = time_ref[pl.ds(me, 1), :] * total[:, :rank] / total[:, rank:]

    def send_row(off):
        peer = lax.rem(flat + off, n * m)
        move(
            times_all.at[flat], times_all.at[flat], row_s, row_r, lax.rem(peer, n), peer // n
        ).start()

    loop(1, n * m, send_row)
    all_of(halves.at[others], half_s, half_r).wait_recv()
    mine = pl.ds(tm * n, n)
    fwd_copy = move(halves.at[mine], halves.at[mine], fwd_s, fwd_r, me, other)
    fwd_copy.start()
    wide_copy.wait_recv()
    flip(wide_in, 1)

    all_of(parts_in.at[others], part_s, part_r).wait_send()
    all_of(halves.at[others], half_s, half_r).wait_send()
    wide_copy.wait_send()
    all_of(times_all.at[pl.ds(1, n * m - 1)], row_s, row_r).wait_recv()
    for k in range(n * m):
        times_flat[k:k + 1, :] = times_all[k]

    weights = []
    for index in (tm, other):
        low = times_flat[aligned(index, kk), :].astype(BF16).astype(F32)
        weights.extend(low * runs[i:i + 1] for i in range(rows))
    weight = jnp.concatenate(split(jnp.concatenate(weights, axis=0)), axis=1)

    def send_term(index):
        peer = ahead(index)
        move(terms.at[peer], terms_in.at[index], term_s, term_r, peer, tm).start()

    for k in list(range(1, zs)) + [0]:
        to_z = lax.rem(z + k, zs)
        piece = flipped[aligned(to_z, strip), :]
        terms[pl.ds(to_z * QUAD, QUAD)] = fold(dot_low(piece, weight)).reshape(QUAD, block, rank)
        loop(max(k * QUAD, 1), (k + 1) * QUAD, send_term, QUAD if k else QUAD - 1)
    all_of(times_all.at[pl.ds(1, n * m - 1)], row_s, row_r).wait_send()
    fwd_copy.wait()
    run_gram = self_gram(halves[...].reshape(n * m * half, rank))
    time_gram = self_gram(times_flat[...])
    own = bin_ref[aligned(flat, block), :]
    scale = own / dot_f32(own, run_gram * time_gram)

    def narrow(i):
        slabs[1, aligned(i, chunk), :] = wide_in[aligned(i, chunk), :].astype(BF16)

    loop(0, 8, narrow)
    gram_sum[...] = jnp.zeros_like(gram_sum)
    inner_sum[...] = jnp.zeros_like(inner_sum)
    total = terms[me]
    all_of(terms_in.at[others], term_s, term_r).wait_recv()
    for index in range(1, n):
        total = total + terms_in[index]
    bins_all[flat] = scale * total

    def send_bins(index):
        move(
            bins_all.at[flat], bins_all.at[flat], bin_s, bin_r.at[index // QUAD], ahead(index), tm
        ).start()

    loop(1, n, send_bins, 5 if n % 5 == 1 else 1)
    all_of(terms_in.at[others], term_s, term_r).wait_send()

    def group(core, k):
        return pl.ds(core * n + lax.rem(z - k + zs, zs) * QUAD, QUAD)

    def hand_on(k):
        mine = bins_all.at[group(tm, k)]
        move(mine, mine, pass_s, pass_r.at[k], me, other).start()

    all_of(bins_all.at[pl.ds(0, QUAD - 1)], bin_s, bin_r.at[0]).wait_recv()
    hand_on(0)

    def arrive(k):
        all_of(bins_all.at[group(tm, k)], bin_s, bin_r.at[k]).wait_recv()
        hand_on(k)

    loop(1, zs, arrive)

    def use(k):
        from_z = lax.rem(z - k + zs, zs)
        all_of(bins_all.at[group(other, k)], pass_s, pass_r.at[k]).wait_recv()
        pieces = []
        for core in range(m):
            mine = group(core, k)
            pieces.append(bins_all[mine].reshape(strip, rank))
            pltpu.make_async_copy(bins_all.at[mine], bin_out.at[mine], out_sem.at[k, core]).start()
        bins = jnp.concatenate(pieces, axis=0)
        bins_low = bins.astype(BF16)
        gram_sum[...] += self_gram(bins)
        for off in range(m):
            slab = jnp.concatenate(
                [slabs[off, :, aligned(core * zs + from_z, strip)] for core in range(m)], axis=1
            )
            inner_sum[off] += dot_low(slab, bins_low)

    loop(0, zs, use)
    run_terms = None
    for off, index in enumerate((tm, other)):
        weight = times_flat[aligned(index, kk), :]
        some = jnp.sum(inner_sum[off].reshape(rows, kk, rank) * weight[None], axis=1)
        run_terms = some if run_terms is None else run_terms + some
    run_out[...] = runs * run_terms / (dot_f32(runs, gram_sum[...] * time_gram) + 1.0 - live)
    time_out[...] = times_flat[aligned(tm, kk), :]
    all_of(bins_all.at[others], bin_s, bin_r.at[0]).wait_send()
    all_of(bins_all.at[mine], pass_s, pass_r.at[0]).wait_send()

    def finish(k):
        for core in range(m):
            mine = group(core, k)
            pltpu.make_async_copy(bins_all.at[mine], bin_out.at[mine], out_sem.at[k, core]).wait()

    loop(0, zs, finish)


def hand_out(run_in, bin_in, time_in, run_out, bin_out, time_out, runs, bins, times, in_s, out_s):
    size = bins.shape[0] // QUAD
    moves = [(run_in, runs, run_out), (time_in, times, time_out)]
    for index in range(QUAD):
        mine = pl.ds(index * size, size)
        moves.append((bin_in.at[mine], bins.at[mine], bin_out.at[mine]))
    loads = [pltpu.make_async_copy(a, b, in_s.at[i]) for i, (a, b, _) in enumerate(moves)]
    stores = [pltpu.make_async_copy(b, c, out_s.at[i]) for i, (_, b, c) in enumerate(moves)]
    for made in loads:
        made.start()
    for load, store in zip(loads, stores):
        load.wait()
        store.start()
    for made in stores:
        made.wait()


def fused(n, m, tensor, run_counts, run_init, bin_init, time_init):
    rows, kk, jj = tensor.shape
    rank = bin_init.shape[1]
    block = jj // (n * m)
    half = rows // m
    zs = n // QUAD
    dma = pltpu.SemaphoreType.DMA
    vmem = pl.BlockSpec(memory_space=pltpu.VMEM)
    anywhere = pl.BlockSpec(memory_space=pl.ANY)
    shapes = (
        jax.ShapeDtypeStruct((rows, rank), F32),
        jax.ShapeDtypeStruct((n * m, block, rank), F32),
        jax.ShapeDtypeStruct((kk, rank), F32),
    )
    results = pl.pallas_call(
        functools.partial(kernel, n, m),
        out_shape=shapes,
        in_specs=[anywhere] * 5,
        out_specs=(vmem, anywhere, vmem),
        scratch_shapes=[
            pltpu.SMEM((1,), jnp.int32),
            pltpu.VMEM((m, rows * kk, jj), BF16),
            pltpu.VMEM((rows, rank), F32),
            pltpu.VMEM((jj, rank), F32),
            pltpu.VMEM((kk, rank), F32),
            pltpu.VMEM((rows * kk, jj), F32),
            pltpu.VMEM((rows * kk, jj), F32),
            pltpu.VMEM((jj // m, m * rows * kk), BF16),
            pltpu.VMEM((n, block, rank), F32),
            pltpu.VMEM((n, block, rank), F32),
            pltpu.VMEM((n * m, block, rank), F32),
            pltpu.VMEM((m, rows * kk, rank), F32),
            pltpu.VMEM((rank, rank), F32),
            pltpu.VMEM((n * m, half, rank), F32),
            pltpu.VMEM((n, 1, 2 * rank), F32),
            pltpu.VMEM((n, 1, 2 * rank), F32),
            pltpu.VMEM((n * m, 1, rank), F32),
            pltpu.VMEM((n * m, rank), F32),
            dma((5,)), *[dma] * 12, dma, dma((zs,)), dma, dma((zs,)), dma((zs, m)),
        ],
        compiler_params=pltpu.CompilerParams(
            collective_id=0, has_side_effects=True, vmem_limit_bytes=VMEM_LIMIT
        ),
    )(run_counts, tensor.reshape(rows * kk, jj), run_init, bin_init, time_init)
    runs, bins, times = pl.pallas_call(
        hand_out,
        out_shape=shapes,
        in_specs=[anywhere] * 3,
        out_specs=[anywhere] * 3,
        scratch_shapes=[pltpu.VMEM(x.shape, F32) for x in shapes] + [dma((2 + QUAD,))] * 2,
        compiler_params=pltpu.CompilerParams(vmem_limit_bytes=VMEM_LIMIT),
    )(*results)
    return runs, bins.reshape(jj, rank), times


def update(n, m, *args):
    rows, kk, jj = args[0].shape
    fits = m == 2 and kk == n and n % QUAD == 0 and kk % 16 == 0 and rows % (8 * m) == 0
    fits = fits and jj % (8 * n * m) == 0 and (QUAD * jj // (n * m)) % 128 == 0
    return fused(n, m, *args) if fits else shards(*args)


def solution(mesh):
    return jax.shard_map(
        functools.partial(update, mesh.shape["runs"], mesh.shape["tm"]),
        mesh=mesh,
        in_specs=(P("runs", "tm", None), P("runs"), P("runs", None), P(), P("tm", None)),
        out_specs=(P("runs", None), P(), P("tm", None)),
        check_vma=False,
    )
```
